32 devices in a mesh: area: 8 (over z, x), harm: 4 (over y, core).
Axes of the slice: x: 2, y: 2, z: 4, core: 2. Of those that a mesh axis runs over, the one named last changes fastest.
Arguments:
- volt: float32 [2, 8, 28, 32, 768], P(None, 'area', 'harm'), may hold values from -3 to 3
- inject: float32 [2, 8, 28, 32, 768], P(None, 'area', 'harm'), may hold values from -6 to 6
- zinv: bfloat16 [2, 8, 28, 768, 768], P(None, 'area', 'harm')
- dev_bus: int32 [8, 2048], P('area'), may hold values from 0 to 767
- dev_count: int32 [8], P('area'), may hold values from 1 to 2048, 8192 in all
- dev_cond: float32 [8, 2048], P('area'), may hold values from 0.1 to 1
- dev_sat: float32 [8, 2048], P('area'), may hold values from 0.2 to 2
- tie_bus: int32 [8, 256], P('area'), may hold values from 0 to 127
- tie_area: int32 [8, 256, 1], P('area'), may hold values from 0 to 7; in each aligned block of 256 rows (0 to 255, 256 to 511, ..., all dimensions but the last counted through in order) at most 64 rows name the same one
- tie_far: int32 [8, 256], P('area'), may hold values from 0 to 127
- tie_res: float32 [8, 256], P('area'), may hold values from 0.5 to 2
- tie_reac: float32 [8, 256], P('area'), may hold values from 0.01 to 0.1
Outputs:
- volt_next: float32 [2, 8, 28, 32, 768], P(None, 'area', 'harm')
The draws below stay inside these ranges and needn't reach their ends.
Inputs may be any that keep to these rules, and one draw needn't show every extreme that they name: `dev_count`: slot k of an area holds an inverter exactly when k is below its count; the counts sum to 8192 and some area has exactly 2048 inverters. `tie_area`: in one area's list no area is named more than 64 times, and in some list some area is named exactly 64 times; every area is named in some list; a list may name its own area.
All inputs are finite; a program needn't handle non-finite values. No bound on the sum of `dev_count` on one device may be relied on, other than what follows from the above.
Results may differ from the reference program's by a relative error of at most 0.0029.
Values sent between devices are 32-bit elements; how exact they have to be, the bound alone decides.
No kernel may reach another device: no remote copies, remote signals or barrier semaphores. Data moves between devices by JAX's collectives and lax.ppermute only.
A program may use at most 128 MiB of HBM per device.

```python
import math
import jax
import jax.numpy as jnp
import numpy as np
from jax import lax

NB = 768
NBD = 128
H = 28
TS = 512
CAP = 2048
NT = 256
SCEN = 32
AREAS = 8
PEER_CAP = 64


def draw_zinv(key, part):
    key_noise, key_real, key_imag = jax.random.split(key, 3)
    shape = (2, AREAS, H, NB, NB)
    noise_part = jax.random.normal(key_noise, shape, jnp.float32)
    noise_part = noise_part * (0.5 / math.sqrt(NB))
    diag_real = jnp.exp(jax.random.uniform(key_real, (AREAS, H, NB), jnp.float32, math.log(0.5), math.log(2.0)))
    diag_imag = jax.random.uniform(key_imag, (AREAS, H, NB), jnp.float32, -0.5, 0.5)
    diagonal = jnp.stack([diag_real, diag_imag])[..., None]
    row_ids = lax.broadcasted_iota(jnp.int32, (NB, NB), 0)
    col_ids = lax.broadcasted_iota(jnp.int32, (NB, NB), 1)
    on_diagonal = row_ids == col_ids
    return (noise_part + jnp.where(on_diagonal, diagonal, 0.0)).astype(jnp.bfloat16)


def plant(values, key, low, high):
    extent = values.shape
    index_at = [jax.random.randint(jax.random.fold_in(key, axis), (), 0, extent[axis]) for axis in range(len(extent))]
    values = values.at[tuple(index_at)].set(low)
    longest = extent.index(max(extent))
    index_at[longest] = (index_at[longest] + 1) % extent[longest]
    return values.at[tuple(index_at)].set(high)


def shard_levels(key, shape, shards, least, high):
    def one(dim, shards_of):
        heights = jax.random.uniform(jax.random.fold_in(jax.random.fold_in(key, 6), dim), (shards_of,), jnp.float32, least / len(shards), high / len(shards))
        return jnp.repeat(jnp.exp(heights), shape[dim] // shards_of).reshape((-1,) + (1,) * (len(shape) - dim - 1))

    loudness = one(*shards[0])
    for cut in shards[1:]:
        loudness = loudness * one(*cut)
    return loudness


def split_up(number_of, total, most, lean):
    weights = [(1 << 20) // math.isqrt(standing ** lean) + 1 for standing in range(2, number_of + 1)]
    rest, holding = total - most - (number_of - 1), [1] * (number_of - 1)
    while rest > 0:
        movable = [i for i in range(number_of - 1) if holding[i] < most]
        mass, left = sum([weights[i] for i in movable]), rest
        for i in movable:
            extra = min(most - holding[i], max(1, left * weights[i] // mass), rest)
            holding[i] = holding[i] + extra
            rest = rest - extra
    return np.array([most] + holding)


def ragged(own_key, count, total, bound, slope):
    if count == 2:
        one = jax.random.randint(own_key, (), max(1, total - bound), min(bound, total - 1) + 1)
        return jnp.stack([one, total - one])
    lengths = jnp.asarray(split_up(count, total, bound, slope), jnp.int32)
    pairs = (count - 1) // 2
    giver, sink = lengths[1:1 + 2 * pairs:2], lengths[2:2 + 2 * pairs:2]
    margin = jnp.minimum(giver - 1, bound - sink)
    moved = jax.random.randint(jax.random.fold_in(own_key, 1), (pairs,), 0, 1 << 20) % (margin + 1)
    lengths = lengths.at[1:1 + 2 * pairs:2].set(giver - moved).at[2:2 + 2 * pairs:2].set(sink + moved)
    return lengths[jax.random.permutation(jax.random.fold_in(own_key, 2), count)]


def shared_out(stream_key, own, number, rows, count, top, limit, skew):
    ranking = jax.random.permutation(stream_key, count)
    packed, ordinary = shares(count, rows * top, limit, skew, True), shares(count, rows * top, limit, skew, False)
    places = jnp.arange(count)

    def named(sizes, turn):
        used = int((sizes > 0).sum())
        fixed = max(1, used // 4)
        shifted = fixed + (places - fixed + turn * (used - fixed)) % max(1, count - fixed)
        return jnp.zeros((count,), jnp.int32).at[ranking[jnp.where(places < fixed, places, shifted)]].set(jnp.asarray(sizes, jnp.int32))

    sizes = jnp.where(number % 4 == 0, named(packed, number // 4), named(ordinary, number - number // 4 - 1))
    mixed = jax.random.permutation(jax.random.fold_in(own, 3), count)
    source_of, taker = mixed[0:count // 2 * 2:2], mixed[1:count // 2 * 2:2]
    room = jnp.minimum(sizes[source_of] - 1, limit - sizes[taker]) // 2
    room = jnp.where((source_of == ranking[0]) | (taker == ranking[0]) | (sizes[taker] == 0), 0, jnp.maximum(room, 0))
    shifted = jax.random.randint(jax.random.fold_in(own, 4), (count // 2,), 0, 1 << 20) % (room + 1)
    sizes = sizes.at[source_of].add(-shifted).at[taker].add(shifted)
    labels = jnp.searchsorted(jnp.cumsum(sizes), jnp.arange(rows * top), side="right").astype(jnp.int32)
    listing = labels.reshape(top, rows).T
    listing = listing[jax.random.permutation(jax.random.fold_in(own, 1), rows)]
    turn = jax.random.randint(jax.random.fold_in(own, 2), (rows, 1), 0, top)
    return jnp.take_along_axis(listing, (jnp.arange(top)[None, :] + turn) % top, axis=1)


def shares(number_of, total, most, skew, full):
    loads = [(1 << 20) // math.isqrt(rank ** skew) + 1 for rank in range(1, number_of + 1)]
    largest = most if full else min(most, max(-(-total // number_of), total * loads[0] // sum(loads)))
    least = 1 if total - largest >= number_of - 1 else 0
    counts, surplus = [largest] + [least] * (number_of - 1), total - largest - least * (number_of - 1)
    while surplus > 0:
        candidates = [i for i in range(1, number_of) if counts[i] < largest] or [i for i in range(1, number_of) if counts[i] < most]
        whole, left = sum([loads[i] for i in candidates]), surplus
        for i in candidates:
            extra = min(most - counts[i], max(1, left * loads[i] // whole), surplus)
            counts[i] = counts[i] + extra
            surplus = surplus - extra
    return np.array(counts)


def bell_draw(rng, shape, scale, reach, shards=(), kind=jnp.bfloat16):
    level = shard_levels(rng, shape, shards, -0.22, 0.18) if shards else 1.0
    array = jax.random.normal(rng, shape, jnp.float32) * scale * level
    return jnp.minimum(jnp.maximum(array, -reach), reach).astype(kind)


def setup_inputs(seed: int = 0) -> dict:
    streams_of = jax.random.split(jax.random.key(seed), 13)
    volt = bell_draw(streams_of[0], (2, AREAS, H, SCEN, NB), 0.5, 3.0, ((1, 8), (2, 4)), jnp.float32)
    inject = bell_draw(streams_of[1], (2, AREAS, H, SCEN, NB), 1.0, 6.0, ((1, 8), (2, 4)), jnp.float32)
    zinv = draw_zinv(jax.random.fold_in(streams_of[12], 71), 0)
    dev_bus = plant(jax.random.randint(streams_of[3], (AREAS, CAP), 0, NB), jax.random.fold_in(streams_of[3], 1), 0, NB - 1).astype(jnp.int32)
    dev_count = ragged(streams_of[4], AREAS, AREAS * CAP // 2, CAP, 2).astype(jnp.int32)
    dev_cond = jnp.clip(jnp.exp(math.log(1.0) - 2.3025851 * jax.random.uniform(streams_of[5], (AREAS, CAP), jnp.float32) ** shard_levels(streams_of[5], (AREAS, CAP), ((0, 8),), -0.2, 0.2)), 0.1, 1.0)
    dev_sat = jnp.clip(jnp.exp(math.log(2.0) - 2.3025851 * jax.random.uniform(streams_of[6], (AREAS, CAP), jnp.float32) ** shard_levels(streams_of[6], (AREAS, CAP), ((0, 8),), -0.2, 0.2)), 0.2, 2.0)
    tie_bus = plant(jax.random.randint(streams_of[7], (AREAS, NT), 0, NBD), jax.random.fold_in(streams_of[7], 1), 0, NBD - 1).astype(jnp.int32)
    tie_area_keys = jax.random.split(jax.random.fold_in(streams_of[8], 1), AREAS * NT // NT)
    tie_area_turns = jax.random.permutation(jax.random.fold_in(streams_of[8], 3), AREAS * NT // NT)
    tie_area = jax.vmap(lambda own, number: shared_out(jax.random.fold_in(streams_of[8], 2), own, number, NT, AREAS, 1, PEER_CAP, 2))(tie_area_keys, tie_area_turns).reshape((AREAS, NT, 1))
    tie_far = plant(jax.random.randint(streams_of[9], (AREAS, NT), 0, NBD), jax.random.fold_in(streams_of[9], 1), 0, NBD - 1).astype(jnp.int32)
    tie_res = jnp.clip(jnp.exp(math.log(2.0) - 1.3862944 * jax.random.uniform(streams_of[10], (AREAS, NT), jnp.float32) ** shard_levels(streams_of[10], (AREAS, NT), ((0, 8),), -0.2, 0.2)), 0.5, 2.0)
    tie_reac = jnp.clip(jnp.exp(math.log(0.1) - 2.3025851 * jax.random.uniform(streams_of[11], (AREAS, NT), jnp.float32) ** shard_levels(streams_of[11], (AREAS, NT), ((0, 8),), -0.2, 0.2)), 0.01, 0.1)
    return {"volt": volt, "inject": inject, "zinv": zinv, "dev_bus": dev_bus, "dev_count": dev_count, "dev_cond": dev_cond, "dev_sat": dev_sat, "tie_bus": tie_bus, "tie_area": tie_area, "tie_far": tie_far, "tie_res": tie_res, "tie_reac": tie_reac}


HIGH = lax.Precision.HIGHEST


def phase_table(first_row, row_count):
    sample_ids = jnp.arange(TS, dtype=jnp.int32)[:, None]
    orders = 2 * (first_row + jnp.arange(row_count, dtype=jnp.int32)) + 1
    phase_turns = (sample_ids * orders[None, :]) % TS
    angles = phase_turns.astype(jnp.float32) * (2.0 * math.pi / TS)
    return jnp.cos(angles), jnp.sin(angles)


def reference(volt, inject, zinv, dev_bus, dev_count, dev_cond, dev_sat, tie_bus, tie_area, tie_far, tie_res, tie_reac):
    cosine_table, sine_table = phase_table(0, H)
    orders = (2 * jnp.arange(H, dtype=jnp.int32) + 1).astype(jnp.float32)
    bus_ids = jnp.arange(NB, dtype=jnp.int32)
    edge_ids = jnp.arange(NBD, dtype=jnp.int32)
    slot_ids = jnp.arange(CAP, dtype=jnp.int32)

    def one_area(area_index):
        volt_area = lax.dynamic_index_in_dim(volt, area_index, 1, keepdims=False)
        inject_area = lax.dynamic_index_in_dim(inject, area_index, 1, keepdims=False)
        zinv_area = lax.dynamic_index_in_dim(zinv, area_index, 1, keepdims=False).astype(jnp.float32)
        dev_buses = dev_bus[area_index]
        live_slot = (slot_ids < dev_count[area_index]).astype(jnp.float32)
        dev_volt = jnp.take(volt_area, dev_buses, axis=3)
        waveform = jnp.einsum("th,hsk->tsk", cosine_table, dev_volt[0], precision=HIGH) - jnp.einsum("th,hsk->tsk", sine_table, dev_volt[1], precision=HIGH)
        current = (dev_cond[area_index] * live_slot) * waveform + (dev_sat[area_index] * live_slot) * jnp.tanh(2.0 * waveform)
        harm_real = (2.0 / TS) * jnp.einsum("th,tsk->hsk", cosine_table, current, precision=HIGH)
        harm_imag = -(2.0 / TS) * jnp.einsum("th,tsk->hsk", sine_table, current, precision=HIGH)
        onehot = (dev_buses[:, None] == bus_ids[None, :]).astype(jnp.float32)
        bus_real = jnp.einsum("hsk,kb->hsb", harm_real, onehot, precision=HIGH)
        bus_imag = jnp.einsum("hsk,kb->hsb", harm_imag, onehot, precision=HIGH)
        targets = tie_area[area_index, :, 0]
        far_bus = tie_far[area_index]
        far_volt = volt[:, targets, :, :, far_bus]
        resist = tie_res[area_index][:, None]
        reactance = tie_reac[area_index][:, None] * orders[None, :]
        denominator = resist * resist + reactance * reactance
        adm_real = (resist / denominator)[:, :, None]
        adm_imag = (-reactance / denominator)[:, :, None]
        tie_real = adm_real * far_volt[:, 0] - adm_imag * far_volt[:, 1]
        tie_imag = adm_real * far_volt[:, 1] + adm_imag * far_volt[:, 0]
        tie_onehot = (tie_bus[area_index][:, None] == edge_ids[None, :]).astype(jnp.float32)
        tie_real_sum = jnp.einsum("ths,tb->hsb", tie_real, tie_onehot, precision=HIGH)
        tie_imag_sum = jnp.einsum("ths,tb->hsb", tie_imag, tie_onehot, precision=HIGH)
        padding = jnp.zeros((H, SCEN, NB - NBD), jnp.float32)
        rhs_real = (inject_area[0] + bus_real + jnp.concatenate([tie_real_sum, padding], axis=2)).astype(jnp.bfloat16)
        rhs_imag = (inject_area[1] + bus_imag + jnp.concatenate([tie_imag_sum, padding], axis=2)).astype(jnp.bfloat16)
        rhs_real = lax.optimization_barrier(rhs_real).astype(jnp.float32)
        rhs_imag = lax.optimization_barrier(rhs_imag).astype(jnp.float32)
        next_real = jnp.einsum("hij,hsj->hsi", zinv_area[0], rhs_real, precision=HIGH) - jnp.einsum("hij,hsj->hsi", zinv_area[1], rhs_imag, precision=HIGH)
        next_imag = jnp.einsum("hij,hsj->hsi", zinv_area[0], rhs_imag, precision=HIGH) + jnp.einsum("hij,hsj->hsi", zinv_area[1], rhs_real, precision=HIGH)
        return jnp.stack([next_real, next_imag])

    result = lax.map(one_area, jnp.arange(AREAS, dtype=jnp.int32))
    return jnp.moveaxis(result, 0, 1)
```

```python
import functools

import jax
import jax.numpy as jnp
import numpy as np
from jax import lax
from jax.experimental import pallas as pl
from jax.experimental.pallas import tpu as pltpu
from jax.sharding import PartitionSpec as P

TS = 512
HALF = TS // 2
NBD = 128
LANES = 128
BF16 = jnp.bfloat16
F32 = jnp.float32
NT_DIMS = (((1,), (1,)), ((), ()))
VMEM_BYTES = 40 * 1024 * 1024


def up(value, step):
    return -(-value // step) * step


def split(value):
    high = value.astype(BF16)
    return high, (value - high.astype(F32)).astype(BF16)


def np_split(value):
    value = np.asarray(value, np.float32)
    high = value.astype(jnp.bfloat16)
    return high, (value - high.astype(np.float32)).astype(jnp.bfloat16)


def chunk_sizes(buses):
    sizes = []
    left = buses
    while left > 0:
        sizes.append(min(256, left))
        left -= sizes[-1]
    return sizes


def wave_tables(ranks, h_local):
    order_count = ranks * h_local
    samples = np.arange(HALF)[:, None]
    orders = 2 * np.arange(order_count)[None, :] + 1
    angles = (samples * orders % TS) * (2.0 * np.pi / TS)
    cos, sin = np.cos(angles), np.sin(angles)
    rows = 2 * h_local
    k_pad = up(ranks * rows, 16)
    m_pad = up(rows, 8)
    forward, inverse = [], []
    for rank in range(ranks):
        there = np.zeros((HALF, k_pad))
        back = np.zeros((2 * m_pad, HALF))
        for k in range(ranks):
            own = slice((rank ^ k) * h_local, ((rank ^ k) + 1) * h_local)
            part = np.concatenate([cos[:, own], -sin[:, own]], axis=1)
            there[:, k * rows : (k + 1) * rows] = 2.0 * part
            if k < 2:
                back[k * m_pad : k * m_pad + rows] = (4.0 / TS) * part.T
        high, low = np_split(there)
        forward.append(np.concatenate([high, high, low], axis=1))
        high, low = np_split(back)
        inverse.append(np.concatenate([high, low], axis=0))
    return np.stack(forward), np.stack(inverse), k_pad, m_pad


def wave_kernel(
    scens, rows, k_pad, m_pad, rank_ref, there_ref, back_ref, *refs
):
    sources = refs[:-4]
    own_ref, sib_ref, buf, sems = refs[-4:]
    block = rows * scens
    columns = buf.shape[0]
    copies = []
    for k, source in enumerate(sources):
        for j in range(columns):
            copy = pltpu.make_async_copy(
                source.at[:, pl.ds(j * LANES, LANES)],
                buf.at[j, pl.ds(k * block, block)],
                sems.at[k, j],
            )
            copy.start()
            copies.append(copy)
    used = len(sources) * block
    if k_pad * scens > used:
        buf[:, pl.ds(used, k_pad * scens - used), :] = jnp.zeros(
            (columns, k_pad * scens - used, LANES), F32
        )
    for copy in copies:
        copy.wait()
    for s in range(scens):
        volts = [buf[j, pl.ds(s, k_pad, stride=scens), :] for j in range(columns)]
        high, low = split(jnp.concatenate(volts, axis=1))
        stacked = jnp.concatenate([high, low, high], axis=0)
        wave = jnp.dot(there_ref[0], stacked, preferred_element_type=F32)
        shaped = jnp.tanh(wave.astype(BF16))
        out = jnp.dot(back_ref[0], shaped, preferred_element_type=F32)
        out = out[: 2 * m_pad] + out[2 * m_pad :]
        for j in range(columns):
            at = slice(j * LANES, (j + 1) * LANES)
            own_ref[j, pl.ds(s * m_pad, m_pad), :] = out[:m_pad, at]
            sib_ref[j, pl.ds(s * m_pad, m_pad), :] = out[m_pad:, at]


def wave(rank, tables, sources, scens, rows):
    there, back, k_pad, m_pad = tables
    width = sources[0].shape[1]
    ranks = len(sources)
    columns = width // LANES
    shape = jax.ShapeDtypeStruct((columns, scens * m_pad, LANES), F32)
    grid_spec = pltpu.PrefetchScalarGridSpec(
        num_scalar_prefetch=1,
        grid=(1,),
        in_specs=[
            pl.BlockSpec((1,) + there.shape[1:], lambda i, r: (r[0], 0, 0)),
            pl.BlockSpec((1,) + back.shape[1:], lambda i, r: (r[0], 0, 0)),
        ]
        + [pl.BlockSpec(memory_space=pl.ANY)] * ranks,
        out_specs=[pl.BlockSpec(shape.shape, lambda i, r: (0, 0, 0))] * 2,
        scratch_shapes=[
            pltpu.VMEM((columns, k_pad * scens, LANES), F32),
            pltpu.SemaphoreType.DMA((ranks, columns)),
        ],
    )
    return pl.pallas_call(
        functools.partial(wave_kernel, scens, rows, k_pad, m_pad),
        grid_spec=grid_spec,
        out_shape=[shape, shape],
        compiler_params=pltpu.CompilerParams(vmem_limit_bytes=VMEM_BYTES),
        cost_estimate=pl.CostEstimate(
            flops=2 * scens * width * HALF * 512,
            bytes_accessed=4 * width * scens * (k_pad + 2 * m_pad),
            transcendentals=scens * width * HALF,
        ),
        name="wave",
    )(rank, jnp.asarray(there), jnp.asarray(back), *sources)


def level_kernel(buses, step, count_ref, bus_ref, cond_ref, sat_ref, out_ref):
    slots = bus_ref.shape[1]
    total = jnp.zeros((16, buses), F32)
    for start in range(0, slots, step):
        at = pl.ds(start, step)
        slot_ids = lax.broadcasted_iota(jnp.int32, (1, step), 1) + start
        live = slot_ids < count_ref[0]
        pieces = []
        for ref in (cond_ref, sat_ref):
            rest = jnp.where(live, ref[:, at], 0.0)
            for _ in range(3):
                high = rest.astype(BF16).astype(F32)
                pieces.append(high)
                rest = rest - high
        pieces.append(jnp.zeros((10, step), F32))
        weights = jnp.concatenate(pieces, axis=0).astype(BF16)
        bus_ids = lax.broadcasted_iota(jnp.int32, (buses, step), 0)
        onehot = jnp.where(bus_ids == bus_ref[:, at], 1.0, 0.0).astype(BF16)
        total += lax.dot_general(
            weights, onehot, NT_DIMS, preferred_element_type=F32
        )
    out_ref[0:1, :] = total[0:1] + total[1:2] + total[2:3]
    out_ref[1:2, :] = total[3:4] + total[4:5] + total[5:6]


def levels(dev_count, dev_bus, dev_cond, dev_sat, buses):
    slots = dev_bus.shape[1]
    step = 512 if slots % 512 == 0 else slots
    return pl.pallas_call(
        functools.partial(level_kernel, buses, step),
        in_specs=[
            pl.BlockSpec(memory_space=pltpu.SMEM),
            pl.BlockSpec(memory_space=pltpu.VMEM),
            pl.BlockSpec(memory_space=pltpu.VMEM),
            pl.BlockSpec(memory_space=pltpu.VMEM),
        ],
        out_specs=pl.BlockSpec(memory_space=pltpu.VMEM),
        out_shape=jax.ShapeDtypeStruct((8, buses), F32),
        compiler_params=pltpu.CompilerParams(vmem_limit_bytes=VMEM_BYTES),
        cost_estimate=pl.CostEstimate(
            flops=2 * 256 * slots * buses, bytes_accessed=16 * slots, transcendentals=0
        ),
        name="levels",
    )(dev_count, dev_bus, dev_cond, dev_sat)


def tie_kernel(
    h_local, scens, id_ref, bus_ref, area_ref, far_ref, res_ref, reac_ref, *refs
):
    blocks, out_ref, scaled = refs[:-2], refs[-2], refs[-1]
    ties = bus_ref.shape[1]
    edge_ids = lax.broadcasted_iota(jnp.int32, (NBD, ties), 0)
    far_hit = edge_ids == far_ref[...]
    far = jnp.zeros((2 * h_local * scens, ties), F32)
    for first in range(0, len(blocks), 2):
        pair = range(first, min(first + 2, len(blocks)))
        parts = [split(blocks[q][...]) for q in pair]
        onehot = jnp.concatenate(
            [
                jnp.where(far_hit & (area_ref[...] == id_ref[1 + q]), 1.0, 0.0)
                for q in pair
            ],
            axis=0,
        ).astype(BF16)
        for piece in range(2):
            edges = jnp.concatenate([part[piece] for part in parts], axis=1)
            far += jnp.dot(edges, onehot, preferred_element_type=F32)
    resist = res_ref[...]
    imag_rows = h_local * scens
    for h in range(h_local):
        order = (2 * (id_ref[0] * h_local + h) + 1).astype(F32)
        reactance = reac_ref[...] * order
        denominator = resist * resist + reactance * reactance
        adm_real = resist / denominator
        adm_imag = -reactance / denominator
        real = far[h * scens : (h + 1) * scens]
        imag = far[imag_rows + h * scens : imag_rows + (h + 1) * scens]
        scaled[pl.ds(h * scens, scens), :] = adm_real * real - adm_imag * imag
        scaled[pl.ds(imag_rows + h * scens, scens), :] = (
            adm_real * imag + adm_imag * real
        )
    target = jnp.where(edge_ids == bus_ref[...], 1.0, 0.0).astype(BF16)
    high, low = split(scaled[...])
    out_ref[...] = lax.dot_general(
        high, target, NT_DIMS, preferred_element_type=F32
    ) + lax.dot_general(low, target, NT_DIMS, preferred_element_type=F32)


def tie_currents(ids, tie_lists, blocks, h_local, scens):
    ties = tie_lists[0].shape[1]
    rows = 2 * h_local * scens
    vmem = pl.BlockSpec(memory_space=pltpu.VMEM)
    return pl.pallas_call(
        functools.partial(tie_kernel, h_local, scens),
        in_specs=[pl.BlockSpec(memory_space=pltpu.SMEM)]
        + [vmem] * (len(tie_lists) + len(blocks)),
        out_specs=vmem,
        out_shape=jax.ShapeDtypeStruct((rows, NBD), F32),
        scratch_shapes=[pltpu.VMEM((rows, ties), F32)],
        compiler_params=pltpu.CompilerParams(vmem_limit_bytes=VMEM_BYTES),
        cost_estimate=pl.CostEstimate(
            flops=4 * rows * ties * NBD * (len(blocks) + 1),
            bytes_accessed=4 * rows * NBD * (len(blocks) + 1),
            transcendentals=0,
        ),
        name="ties",
    )(ids, *tie_lists, *blocks)


def solve_kernel(
    scens, h_local, m_pad, start, has_tie, has_total, rank_ref, *refs
):
    half = scens // 2
    refs = list(refs)
    volt_ref, inject_ref, zinv_ref, level_ref, own_ref, sib_ref = refs[:6]
    del refs[:6]
    tie_ref = refs.pop(0) if has_tie else None
    total_ref = refs.pop(0) if has_total else None
    (out_ref,) = refs
    h = pl.program_id(0)
    even = rank_ref[0] % 2 == 0
    cond_level = level_ref[0:1, :]
    sat_level = level_ref[1:2, :]
    parts = []
    for c in range(2):
        at = pl.ds(c * h_local + h, half, stride=m_pad)
        own = jnp.concatenate(
            [own_ref[j, at, :] for j in range(own_ref.shape[0])], axis=1
        )
        sib = jnp.concatenate(
            [sib_ref[j, at, :] for j in range(sib_ref.shape[0])], axis=1
        )
        shaped = jnp.concatenate(
            [jnp.where(even, own, sib), jnp.where(even, sib, own)], axis=0
        )
        rhs = inject_ref[c, 0, 0] + (
            cond_level * volt_ref[c, 0, 0] + sat_level * shaped
        )
        if has_tie:
            ties = tie_ref[c, 0]
            if rhs.shape[1] > NBD:
                rhs = jnp.concatenate([rhs[:, :NBD] + ties, rhs[:, NBD:]], axis=1)
            else:
                rhs = rhs + ties
        parts.append(rhs.astype(BF16))
    both = jnp.concatenate(parts, axis=0)
    by_real = lax.dot_general(
        both, zinv_ref[0, 0, 0], NT_DIMS, preferred_element_type=F32
    )
    by_imag = lax.dot_general(
        both, zinv_ref[1, 0, 0], NT_DIMS, preferred_element_type=F32
    )
    real = by_real[:scens] - by_imag[scens:]
    imag = by_real[scens:] + by_imag[:scens]
    if has_total:
        real = real + total_ref[0, 0, 0]
        imag = imag + total_ref[1, 0, 0]
    out_ref[0, 0, 0] = real
    out_ref[1, 0, 0] = imag


def solve(rank, volt, inject, zinv, level, own, sib, tie, total, start, width, m_pad):
    _, _, h_local, scens, buses = volt.shape
    at = start // width
    assert at * width == start
    wide = pl.BlockSpec((2, 1, 1, scens, width), lambda h, r: (0, 0, h, 0, at))
    whole = pl.BlockSpec((2, 1, 1, scens, buses), lambda h, r: (0, 0, h, 0, 0))
    in_specs = [
        wide,
        wide,
        pl.BlockSpec((2, 1, 1, buses, width), lambda h, r: (0, 0, h, 0, at)),
        pl.BlockSpec((8, width), lambda h, r: (0, at)),
        pl.BlockSpec(own.shape, lambda h, r: (0, 0, 0)),
        pl.BlockSpec(sib.shape, lambda h, r: (0, 0, 0)),
    ]
    operands = [volt, inject, zinv, level, own, sib]
    if tie is not None:
        in_specs.append(pl.BlockSpec((2, 1, scens, NBD), lambda h, r: (0, h, 0, 0)))
        operands.append(tie)
    aliases = {}
    if total is not None:
        aliases = {1 + len(operands): 0}
        in_specs.append(whole)
        operands.append(total)
    return pl.pallas_call(
        functools.partial(
            solve_kernel,
            scens,
            h_local,
            m_pad,
            start,
            tie is not None,
            total is not None,
        ),
        grid_spec=pltpu.PrefetchScalarGridSpec(
            num_scalar_prefetch=1, grid=(h_local,), in_specs=in_specs, out_specs=whole
        ),
        out_shape=jax.ShapeDtypeStruct(volt.shape, F32),
        input_output_aliases=aliases,
        compiler_params=pltpu.CompilerParams(vmem_limit_bytes=VMEM_BYTES),
        cost_estimate=pl.CostEstimate(
            flops=8 * h_local * scens * buses * width,
            bytes_accessed=4 * h_local * buses * width,
            transcendentals=0,
        ),
        name="solve",
    )(rank, *operands)


def per_device(
    volt,
    inject,
    zinv,
    dev_bus,
    dev_count,
    dev_cond,
    dev_sat,
    tie_bus,
    tie_area,
    tie_far,
    tie_res,
    tie_reac,
):
    _, _, h_local, scens, buses = volt.shape
    ranks = lax.axis_size("harm")
    areas = lax.axis_size("area")
    rank = lax.axis_index("harm")
    area = lax.axis_index("area")
    half = scens // 2
    rows = 2 * h_local
    rank_arg = jnp.full((1,), rank, jnp.int32)
    tables = wave_tables(ranks, h_local)
    m_pad = tables[3]
    side = rank % 2

    def swap(value, k):
        return lax.ppermute(value, "harm", [(i, i ^ k) for i in range(ranks)])

    sizes = chunk_sizes(buses)
    starts = [buses - sum(sizes[: i + 1]) for i in range(len(sizes))]
    arrived = []
    for start, width in zip(starts, sizes):
        lanes = volt[..., start : start + width]
        mine = lax.dynamic_slice_in_dim(lanes, side * half, half, axis=3)
        other = lax.dynamic_slice_in_dim(lanes, (1 - side) * half, half, axis=3)
        mine = mine.reshape(rows * half, width)
        other = other.reshape(rows * half, width)
        arrived.append(
            [mine] + [swap(other if k % 2 else mine, k) for k in range(1, ranks)]
        )

    edge = volt[..., :NBD].reshape(rows * scens, NBD)
    ring = [(a, (a + 2) % areas) for a in range(areas)]
    pairs = [(a, a ^ 1) for a in range(areas)]
    blocks = [edge]
    block_ids = [area]
    for step in range(areas // 2):
        blocks.append(lax.ppermute(blocks[2 * step], "area", pairs))
        block_ids.append((area - 2 * step) % areas ^ 1)
        if step + 1 < areas // 2:
            blocks.append(lax.ppermute(blocks[2 * step], "area", ring))
            block_ids.append((area - 2 * (step + 1)) % areas)
    ids = jnp.stack([rank] + block_ids).astype(jnp.int32)

    level = levels(dev_count, dev_bus, dev_cond, dev_sat, buses)
    tie_lists = [
        tie_bus,
        tie_area[:, :, 0],
        tie_far,
        tie_res,
        tie_reac,
    ]
    tie = tie_currents(ids, tie_lists, blocks, h_local, scens)
    tie = tie.reshape(2, h_local, scens, NBD)

    total = None
    for start, width, sources in zip(starts, sizes, arrived):
        own, for_sib = wave(rank_arg, tables, sources, half, rows)
        sib = swap(for_sib, 1)
        total = solve(
            rank_arg,
            volt,
            inject,
            zinv,
            level,
            own,
            sib,
            tie if start == 0 else None,
            total,
            start,
            width,
            m_pad,
        )
    return total


def solution(mesh):
    wide = P(None, "area", "harm", None, None)
    flat = P("area", None)
    in_specs = (
        wide,
        wide,
        wide,
        flat,
        P("area"),
        flat,
        flat,
        flat,
        P("area", None, None),
        flat,
        flat,
        flat,
    )
    return jax.shard_map(
        per_device, mesh=mesh, in_specs=in_specs, out_specs=wide, check_vma=False
    )
```

```python
import functools

import jax
import jax.numpy as jnp
import numpy as np
from jax import lax
from jax.experimental import pallas as pl
from jax.experimental.pallas import tpu as pltpu
from jax.sharding import PartitionSpec as P

TS = 512
HALF = TS // 2
NBD = 128
LANES = 128
BF16 = jnp.bfloat16
F32 = jnp.float32
NT_DIMS = (((1,), (1,)), ((), ()))
VMEM_BYTES = 10 * 1024 * 1024
SMALL = pl.CostEstimate(flops=1000, bytes_accessed=1000, transcendentals=0)


def up(value, step):
    return -(-value // step) * step


def split(value):
    high = value.astype(BF16)
    return high, (value - high.astype(F32)).astype(BF16)


def np_split(value):
    value = np.asarray(value, np.float32)
    high = value.astype(jnp.bfloat16)
    return high, (value - high.astype(np.float32)).astype(jnp.bfloat16)


def chunk_sizes(buses):
    last = 256 if buses > 256 else buses
    return [buses - last, last] if buses > last else [last]


def after(value, *others):
    return lax.optimization_barrier((value, *others))[0] if others else value


def wave_tables(ranks, h_local):
    order_count = ranks * h_local
    samples = np.arange(HALF)[:, None]
    orders = 2 * np.arange(order_count)[None, :] + 1
    angles = (samples * orders % TS) * (2.0 * np.pi / TS)
    cos, sin = np.cos(angles), np.sin(angles)
    rows = 2 * h_local
    k_pad = up(ranks * rows, 16)
    m_pad = up(rows, 8)
    forward, inverse = [], []
    for rank in range(ranks):
        there = np.zeros((HALF, k_pad))
        back = np.zeros((ranks * m_pad, HALF))
        for k in range(ranks):
            own = slice((rank ^ k) * h_local, ((rank ^ k) + 1) * h_local)
            part = np.concatenate([cos[:, own], -sin[:, own]], axis=1)
            there[:, k * rows : (k + 1) * rows] = 2.0 * part
            back[k * m_pad : k * m_pad + rows] = (4.0 / TS) * part.T
        high, low = np_split(there)
        forward.append(np.concatenate([high, high, low], axis=1))
        high, low = np_split(back)
        inverse.append(np.concatenate([high, low], axis=0))
    return np.stack(forward), np.stack(inverse), k_pad, m_pad


def wave_kernel(
    source_count, start, m_pad, has_fetch, rank_ref, there_ref, back_ref, *refs
):
    refs = list(refs)
    fetch = None
    if has_fetch:
        fetch = pltpu.make_async_copy(
            refs.pop(source_count).at[1], refs.pop(-5), refs.pop()
        )
    sources, outs = refs[:source_count], refs[source_count:-3]
    buf, shapes, sems = refs[-3:]
    ranks = len(outs)
    columns, k_pad, scens, _ = buf.shape
    rows = outs[0].shape[1] // scens
    mine = pl.ds(pl.multiple_of(rank_ref[0] * scens, 8), scens)
    copies = []
    used = 0
    for k, source in enumerate(sources):
        into = pl.ds(used, source.shape[0])
        used += source.shape[0]
        for j in range(columns):
            rows_at = mine if source.shape[1] > scens else pl.ds(0, scens)
            part = source.at[:, rows_at, pl.ds(start + j * LANES, LANES)]
            copy = pltpu.make_async_copy(part, buf.at[j, into], sems.at[k, j])
            copy.start()
            copies.append(copy)
    if fetch is not None:
        fetch.start()
    if k_pad > used:
        buf[:, pl.ds(used, k_pad - used)] = jnp.zeros(
            (columns, k_pad - used, scens, LANES), F32
        )
    for copy in copies:
        copy.wait()
    flat = buf.reshape(columns, k_pad * scens, LANES)
    for s in range(scens):
        volts = [flat[j, pl.ds(s, k_pad, stride=scens), :] for j in range(columns)]
        high, low = split(jnp.concatenate(volts, axis=1))
        stacked = jnp.concatenate([high, low, high], axis=0)
        wave = jnp.dot(there_ref[...], stacked, preferred_element_type=F32)
        shapes[s] = jnp.tanh(wave.astype(BF16))
    for s in range(scens):
        out = jnp.dot(back_ref[...], shapes[s], preferred_element_type=F32)
        out = out[: ranks * m_pad] + out[ranks * m_pad :]
        for k in range(ranks):
            for j in range(columns):
                outs[k][j, pl.ds(s, rows, stride=scens), :] = out[
                    k * m_pad : k * m_pad + rows, j * LANES : (j + 1) * LANES
                ]
    if fetch is not None:
        fetch.wait()


def wave(rank, tables, m_pad, sources, scens, start, width, fetch):
    rows = sources[0].shape[0]
    ranks = sum(source.shape[0] for source in sources) // rows
    columns = width // LANES
    k_pad = tables[0].shape[1] // 3
    fetches = [] if fetch is None else [fetch]
    vmem = pl.BlockSpec(memory_space=pltpu.VMEM)
    shape = jax.ShapeDtypeStruct((columns, rows * scens, LANES), F32)
    return pl.pallas_call(
        functools.partial(
            wave_kernel, len(sources), start, m_pad, fetch is not None
        ),
        in_specs=[pl.BlockSpec(memory_space=pltpu.SMEM), vmem, vmem]
        + [pl.BlockSpec(memory_space=pl.ANY)] * (len(sources) + len(fetches)),
        out_specs=[vmem] * (ranks + len(fetches)),
        out_shape=[pltpu.VMEM(shape.shape, F32)]
        + [shape] * (ranks - 1)
        + [pltpu.VMEM(each.shape[1:], each.dtype) for each in fetches],
        scratch_shapes=[
            pltpu.VMEM((columns, k_pad, scens, LANES), F32),
            pltpu.VMEM((scens, HALF, width), BF16),
            pltpu.SemaphoreType.DMA((len(sources), columns)),
        ]
        + [pltpu.SemaphoreType.DMA for _ in fetches],
        compiler_params=pltpu.CompilerParams(vmem_limit_bytes=VMEM_BYTES),
        cost_estimate=SMALL,
        name="wave",
    )(rank, *tables, *sources, *fetches)


def level_kernel(
    step,
    rank_ref,
    count_ref,
    bus_hbm,
    cond_hbm,
    sat_hbm,
    volt_hbm,
    inject_hbm,
    there_ref,
    back_ref,
    zinv_ref,
    base_ref,
    sat_out,
    there_out,
    back_out,
    zinv_out,
    bus_ref,
    cond_ref,
    sat_ref,
    volt_ref,
    inject_ref,
    sems,
):
    pairs = [
        (bus_hbm, bus_ref),
        (cond_hbm, cond_ref),
        (sat_hbm, sat_ref),
        (volt_hbm, volt_ref),
        (inject_hbm, inject_ref),
        (there_ref.at[rank_ref[0]], there_out),
        (back_ref.at[rank_ref[0]], back_out),
        (zinv_ref.at[0], zinv_out),
    ]
    copies = [
        pltpu.make_async_copy(*pair, sems.at[q]) for q, pair in enumerate(pairs)
    ]
    for copy in copies:
        copy.start()
    for copy in copies[:3]:
        copy.wait()
    slots = bus_ref.shape[1]
    buses = volt_ref.shape[-1]
    total = jnp.zeros((16, buses), F32)
    for start in range(0, slots, step):
        at = pl.ds(start, step)
        slot_ids = lax.broadcasted_iota(jnp.int32, (1, step), 1) + start
        live = slot_ids < count_ref[0]
        pieces = []
        for ref in (cond_ref, sat_ref):
            rest = jnp.where(live, ref[:, at], 0.0)
            for _ in range(3):
                high = rest.astype(BF16).astype(F32)
                pieces.append(high)
                rest = rest - high
        pieces.append(jnp.zeros((10, step), F32))
        weights = jnp.concatenate(pieces, axis=0).astype(BF16)
        bus_ids = lax.broadcasted_iota(jnp.int32, (buses, step), 0)
        onehot = jnp.where(bus_ids == bus_ref[:, at], 1.0, 0.0).astype(BF16)
        total += lax.dot_general(
            weights, onehot, NT_DIMS, preferred_element_type=F32
        )
    cond = total[0:1] + total[1:2] + total[2:3]
    sat = total[3:4] + total[4:5] + total[5:6]
    sat_out[...] = jnp.broadcast_to(sat, sat_out.shape)
    for copy in copies[3:5]:
        copy.wait()
    for row in range(volt_ref.shape[0]):
        base_ref[row] = inject_ref[row] + cond * volt_ref[row]
    for copy in copies[5:]:
        copy.wait()


def levels(rank, dev_count, dev_bus, dev_cond, dev_sat, volt, inject, tables, zinv):
    slots = dev_bus.shape[1]
    buses = volt.shape[-1]
    step = 512 if slots % 512 == 0 else slots
    vmem = pl.BlockSpec(memory_space=pltpu.VMEM)
    smem = pl.BlockSpec(memory_space=pltpu.SMEM)
    anywhere = pl.BlockSpec(memory_space=pl.ANY)
    there, back = tables
    inputs = [
        pltpu.with_memory_space_constraint(each, pltpu.HBM)
        for each in (dev_bus, dev_cond, dev_sat, volt, inject, there, back)
    ] + [zinv]
    return pl.pallas_call(
        functools.partial(level_kernel, step),
        in_specs=[smem] * 2 + [anywhere] * len(inputs),
        out_specs=[vmem] * 5,
        out_shape=[
            pltpu.VMEM(volt.shape, F32),
            pltpu.VMEM((8, buses), F32),
            pltpu.VMEM(there.shape[1:], BF16),
            pltpu.VMEM(back.shape[1:], BF16),
            pltpu.VMEM(zinv.shape[1:], BF16),
        ],
        scratch_shapes=[pltpu.VMEM(each.shape, each.dtype) for each in inputs[:5]]
        + [pltpu.SemaphoreType.DMA((len(inputs),))],
        compiler_params=pltpu.CompilerParams(vmem_limit_bytes=VMEM_BYTES),
        cost_estimate=SMALL,
        name="levels",
    )(rank, dev_count, *inputs)


def tie_kernel(
    h_local, scens, areas, shifts, place_ref, *refs
):
    lists, blocks, out_ref = refs[:5], refs[5:-9], refs[-9]
    bus_ref, area_ref, far_ref, res_ref, reac_ref = refs[-8:-3]
    scaled, held, sems = refs[-3:]
    list_copies = []
    for q, pair in enumerate(zip(lists, refs[-8:-3])):
        copy = pltpu.make_async_copy(*pair, sems.at[len(blocks) + q])
        copy.start()
        list_copies.append(copy)
    copies = []
    for q, block in enumerate(blocks):
        copy = pltpu.make_async_copy(block, held.at[q], sems.at[q])
        copy.start()
        copies.append(copy)
    for copy in list_copies:
        copy.wait()
    ties = bus_ref.shape[1]
    edge_ids = lax.broadcasted_iota(jnp.int32, (NBD, ties), 0)
    far_hit = edge_ids == far_ref[...]
    far = jnp.zeros((2 * h_local * scens, ties), F32)

    def origin(q):
        ringed = (place_ref[1] + areas - shifts[q // 2]) % areas
        return ringed ^ 1 if q % 2 else ringed

    for first in range(0, len(blocks), 2):
        pair = range(first, min(first + 2, len(blocks)))
        for q in pair:
            copies[q].wait()
        parts = [split(held[q]) for q in pair]
        onehot = jnp.concatenate(
            [
                jnp.where(far_hit & (area_ref[...] == origin(q)), 1.0, 0.0)
                for q in pair
            ],
            axis=0,
        ).astype(BF16)
        for piece in range(2):
            edges = jnp.concatenate([part[piece] for part in parts], axis=1)
            far += jnp.dot(edges, onehot, preferred_element_type=F32)
    resist = res_ref[...]
    imag_rows = h_local * scens
    for h in range(h_local):
        order = (2 * (place_ref[0] * h_local + h) + 1).astype(F32)
        reactance = reac_ref[...] * order
        denominator = resist * resist + reactance * reactance
        adm_real = resist / denominator
        adm_imag = -reactance / denominator
        real = far[h * scens : (h + 1) * scens]
        imag = far[imag_rows + h * scens : imag_rows + (h + 1) * scens]
        scaled[pl.ds(h * scens, scens), :] = adm_real * real - adm_imag * imag
        scaled[pl.ds(imag_rows + h * scens, scens), :] = (
            adm_real * imag + adm_imag * real
        )
    target = jnp.where(edge_ids == bus_ref[...], 1.0, 0.0).astype(BF16)
    high, low = split(scaled[...])
    out_ref[...] = lax.dot_general(
        high, target, NT_DIMS, preferred_element_type=F32
    ) + lax.dot_general(low, target, NT_DIMS, preferred_element_type=F32)


def tie_currents(place, tie_lists, blocks, areas, shifts, h_local, scens):
    ties = tie_lists[0].shape[1]
    rows = 2 * h_local * scens
    vmem = pl.BlockSpec(memory_space=pltpu.VMEM)
    return pl.pallas_call(
        functools.partial(tie_kernel, h_local, scens, areas, shifts),
        in_specs=[pl.BlockSpec(memory_space=pltpu.SMEM)]
        + [pl.BlockSpec(memory_space=pl.ANY)] * (len(tie_lists) + len(blocks)),
        out_specs=vmem,
        out_shape=pltpu.VMEM((rows, NBD), F32),
        scratch_shapes=[pltpu.VMEM(each.shape, each.dtype) for each in tie_lists]
        + [
            pltpu.VMEM((rows, ties), F32),
            pltpu.VMEM((len(blocks), rows, NBD), F32),
            pltpu.SemaphoreType.DMA((len(blocks) + len(tie_lists),)),
        ],
        compiler_params=pltpu.CompilerParams(vmem_limit_bytes=VMEM_BYTES),
        cost_estimate=SMALL,
        name="ties",
    )(place, *tie_lists, *blocks)


def solve_kernel(start, width, has_tie, has_total, ranks, rank_ref, *refs):
    refs = list(refs)
    base_ref, sat_ref, real_ref, imag_ref = refs[:4]
    shaped_refs = refs[4 : 4 + ranks]
    del refs[: 4 + ranks]
    tie_ref = refs.pop(0) if has_tie else None
    total_ref = refs.pop(0) if has_total else None
    out_ref, full = refs[:2]
    refs = refs[2:]
    lanes = pl.ds(start, width)
    stage, sem = refs if has_total else (out_ref, None)
    _, h_local, scens, _ = base_ref.shape
    columns = shaped_refs[0].shape[0]
    part = scens // ranks
    for k, ref in enumerate(shaped_refs):
        quarter = pl.ds(pl.multiple_of((rank_ref[0] ^ k) * part, 8), part)
        for j in range(columns):
            at = pl.ds(j * LANES, LANES)
            for row in range(2 * h_local):
                full[row, quarter, at] = ref[j, pl.ds(row * part, part), :]
    sat = sat_ref[0:1, lanes]
    copies = []
    for h in range(h_local):
        parts = []
        for c in range(2):
            rhs = base_ref[c, h, :, lanes] + sat * full[c * h_local + h]
            if has_tie:
                ties = tie_ref[c, h]
                if width > NBD:
                    rhs = jnp.concatenate([rhs[:, :NBD] + ties, rhs[:, NBD:]], axis=1)
                else:
                    rhs = rhs + ties
            parts.append(rhs.astype(BF16))
        both = jnp.concatenate(parts, axis=0)
        by_real = lax.dot_general(
            both, real_ref[h, :, lanes], NT_DIMS, preferred_element_type=F32
        )
        by_imag = lax.dot_general(
            both, imag_ref[h, :, lanes], NT_DIMS, preferred_element_type=F32
        )
        real = by_real[:scens] - by_imag[scens:]
        imag = by_real[scens:] + by_imag[:scens]
        if has_total:
            real = real + total_ref[0, h]
            imag = imag + total_ref[1, h]
        stage[0, h] = real
        stage[1, h] = imag
        if sem is not None:
            copy = pltpu.make_async_copy(stage.at[:, h], out_ref.at[:, h], sem.at[h])
            copy.start()
            copies.append(copy)
    for copy in copies:
        copy.wait()


def solve(rank, base, sat, zinvs, shaped, tie, total, start, width):
    _, h_local, scens, _ = base.shape
    ranks = len(shaped)
    vmem = pl.BlockSpec(memory_space=pltpu.VMEM)
    operands = [base, sat, *zinvs] + list(shaped)
    operands += [tie] if tie is not None else []
    operands += [total] if total is not None else []
    scratch = [pltpu.VMEM((2 * h_local, scens, width), F32)]
    out_spec = vmem
    if total is not None:
        out_spec = pl.BlockSpec(memory_space=pl.ANY)
        scratch += [
            pltpu.VMEM(base.shape, F32),
            pltpu.SemaphoreType.DMA((h_local,)),
        ]
    return pl.pallas_call(
        functools.partial(
            solve_kernel, start, width, tie is not None, total is not None, ranks
        ),
        in_specs=[pl.BlockSpec(memory_space=pltpu.SMEM), vmem, vmem]
        + [vmem] * (len(operands) - 2),
        out_specs=out_spec,
        out_shape=jax.ShapeDtypeStruct(base.shape, F32),
        scratch_shapes=scratch,
        compiler_params=pltpu.CompilerParams(vmem_limit_bytes=VMEM_BYTES),
        cost_estimate=SMALL,
        name="solve",
    )(rank, *operands)


def per_device(
    volt,
    inject,
    zinv,
    dev_bus,
    dev_count,
    dev_cond,
    dev_sat,
    tie_bus,
    tie_area,
    tie_far,
    tie_res,
    tie_reac,
):
    _, _, h_local, scens, buses = volt.shape
    ranks = lax.axis_size("harm")
    areas = lax.axis_size("area")
    rank = lax.axis_index("harm")
    area = lax.axis_index("area")
    part = scens // ranks
    rows = 2 * h_local
    place = jnp.stack([rank, area]).astype(jnp.int32)
    there, back, _, m_pad = wave_tables(ranks, h_local)
    zinv = pltpu.with_memory_space_constraint(zinv[:, 0], pltpu.HBM)
    flat = volt.reshape(rows, scens, buses)

    def swap(value, k):
        return lax.ppermute(value, "harm", [(i, i ^ k) for i in range(ranks)])

    sizes = chunk_sizes(buses)
    starts = [buses - sum(sizes[: i + 1]) for i in range(len(sizes))]

    def piece(k):
        at = (0, (rank ^ k) * part, 0)
        return lax.dynamic_slice(flat, at, (rows, part, buses))

    pieces = [piece(k) for k in range(ranks - 1, 1, -1)]
    flat_now, *pieces = lax.optimization_barrier((flat, *pieces))
    far = [swap(each, ranks - 1 - q) for q, each in enumerate(pieces)]
    sibling = swap(flat_now, 1)
    sources = [flat, sibling] + far[::-1]

    edge = volt[..., :NBD].reshape(rows * scens, NBD)

    def shift(value, step):
        return lax.ppermute(
            value, "area", [(a, (a + step) % areas) for a in range(areas)]
        )

    def exchange(value):
        return lax.ppermute(value, "area", [(a, a ^ 1) for a in range(areas)])

    edge = after(edge, *pieces)
    blocks = [edge, exchange(edge)]
    base, sat, there, back, zinv_real = levels(
        place,
        dev_count,
        after(dev_bus, sibling),
        dev_cond,
        dev_sat,
        flat,
        inject.reshape(flat.shape),
        (jnp.asarray(there), jnp.asarray(back)),
        zinv,
    )
    def run_wave(index):
        return wave(
            place,
            (there, back),
            m_pad,
            sources,
            part,
            starts[index],
            sizes[index],
            zinv if index == len(sizes) - 1 else None,
        )

    waves = [list(run_wave(index)) for index in range(len(sizes))]
    zinv_imag = waves[-1].pop()
    shaped = [
        [outs[0]] + [swap(outs[k], k) for k in range(1, ranks)] for outs in waves
    ]
    ring = {2: shift(edge, 2)}
    if areas > 4:
        ring[areas - 2] = shift(edge, areas - 2)
    for step in range(4, areas - 2, 2):
        ring[step] = shift(after(ring[step - 2], sat), 2)
    shifts = [0]
    for step, block in ring.items():
        if step == 2:
            needs = [blocks[-1], far[0], sat]
        else:
            needs = blocks[-1:] if step == areas - 2 else [waves[-1][0]]
        blocks += [block, exchange(after(block, *needs))]
        shifts.append(step)
    base = base.reshape(2, h_local, scens, buses)
    tie_lists = [
        tie_bus,
        tie_area[:, :, 0],
        tie_far,
        tie_res,
        tie_reac,
    ]
    tie_lists = [pltpu.with_memory_space_constraint(t, pltpu.HBM) for t in tie_lists]
    tie = tie_currents(place, tie_lists, blocks, areas, shifts, h_local, scens)
    tie = tie.reshape(2, h_local, scens, NBD)

    total = None
    for start, width, parts in zip(starts, sizes, shaped):
        total = solve(
            place,
            base,
            sat,
            (zinv_real, zinv_imag),
            parts,
            tie if start == 0 else None,
            total,
            start,
            width,
        )
    return total[:, None]


def solution(mesh):
    wide = P(None, "area", "harm", None, None)
    flat = P("area", None)
    in_specs = (
        wide,
        wide,
        wide,
        flat,
        P("area"),
        flat,
        flat,
        flat,
        P("area", None, None),
        flat,
        flat,
        flat,
    )
    return jax.shard_map(
        per_device, mesh=mesh, in_specs=in_specs, out_specs=wide, check_vma=False
    )
```

```python
import functools

import jax
import jax.numpy as jnp
import numpy as np
from jax import lax
from jax.experimental import pallas as pl
from jax.experimental.pallas import tpu as pltpu
from jax.sharding import PartitionSpec as P

TS = 512
HALF = TS // 2
NBD = 128
LANES = 128
BF16 = jnp.bfloat16
F32 = jnp.float32
NT_DIMS = (((1,), (1,)), ((), ()))
VMEM_BYTES = 10 * 1024 * 1024
SMALL = pl.CostEstimate(flops=1000, bytes_accessed=1000, transcendentals=0)


def up(value, step):
    return -(-value // step) * step


def split(value):
    high = value.astype(BF16)
    return high, (value - high.astype(F32)).astype(BF16)


def np_split(value):
    value = np.asarray(value, np.float32)
    high = value.astype(jnp.bfloat16)
    return high, (value - high.astype(np.float32)).astype(jnp.bfloat16)


def chunk_sizes(buses):
    last = 256 if buses > 256 else buses
    return [buses - last, last] if buses > last else [last]


def after(value, *others):
    return lax.optimization_barrier((value, *others))[0] if others else value


def wave_tables(ranks, h_local):
    order_count = ranks * h_local
    samples = np.arange(HALF)[:, None]
    orders = 2 * np.arange(order_count)[None, :] + 1
    angles = (samples * orders % TS) * (2.0 * np.pi / TS)
    cos, sin = np.cos(angles), np.sin(angles)
    rows = 2 * h_local
    k_pad = up(ranks * rows, 16)
    m_pad = up(rows, 8)
    forward, inverse = [], []
    for rank in range(ranks):
        there = np.zeros((HALF, k_pad))
        back = np.zeros((ranks * m_pad, HALF))
        for k in range(ranks):
            own = slice((rank ^ k) * h_local, ((rank ^ k) + 1) * h_local)
            part = np.concatenate([cos[:, own], -sin[:, own]], axis=1)
            there[:, k * rows : (k + 1) * rows] = 2.0 * part
            back[k * m_pad : k * m_pad + rows] = (4.0 / TS) * part.T
        high, low = np_split(there)
        forward.append(np.concatenate([high, high, low], axis=1))
        high, low = np_split(back)
        inverse.append(np.concatenate([high, low], axis=0))
    return np.stack(forward), np.stack(inverse), k_pad, m_pad


def wave_kernel(source_count, start, m_pad, rank_ref, there_ref, back_ref, *refs):
    sources, outs = refs[:source_count], refs[source_count:-3]
    buf, shapes, sems = refs[-3:]
    ranks = len(outs)
    columns, k_pad, scens, _ = buf.shape
    rows = outs[0].shape[1] // scens
    mine = pl.ds(pl.multiple_of(rank_ref[0] * scens, 8), scens)
    copies = []
    used = 0
    for k, source in enumerate(sources):
        into = pl.ds(used, source.shape[0])
        used += source.shape[0]
        for j in range(columns):
            rows_at = mine if source.shape[1] > scens else pl.ds(0, scens)
            part = source.at[:, rows_at, pl.ds(start + j * LANES, LANES)]
            copy = pltpu.make_async_copy(part, buf.at[j, into], sems.at[k, j])
            copy.start()
            copies.append(copy)
    if k_pad > used:
        buf[:, pl.ds(used, k_pad - used)] = jnp.zeros(
            (columns, k_pad - used, scens, LANES), F32
        )
    for copy in copies:
        copy.wait()
    flat = buf.reshape(columns, k_pad * scens, LANES)
    for s in range(scens):
        volts = [flat[j, pl.ds(s, k_pad, stride=scens), :] for j in range(columns)]
        high, low = split(jnp.concatenate(volts, axis=1))
        stacked = jnp.concatenate([high, low, high], axis=0)
        wave = jnp.dot(there_ref[...], stacked, preferred_element_type=F32)
        shapes[s] = jnp.tanh(wave.astype(BF16))
    for s in range(scens):
        out = jnp.dot(back_ref[...], shapes[s], preferred_element_type=F32)
        out = out[: ranks * m_pad] + out[ranks * m_pad :]
        for k in range(ranks):
            for j in range(columns):
                outs[k][j, pl.ds(s, rows, stride=scens), :] = out[
                    k * m_pad : k * m_pad + rows, j * LANES : (j + 1) * LANES
                ]


def wave(rank, tables, m_pad, sources, scens, start, width):
    rows = sources[0].shape[0]
    ranks = sum(source.shape[0] for source in sources) // rows
    columns = width // LANES
    k_pad = tables[0].shape[1] // 3
    vmem = pl.BlockSpec(memory_space=pltpu.VMEM)
    shape = jax.ShapeDtypeStruct((columns, rows * scens, LANES), F32)
    return pl.pallas_call(
        functools.partial(wave_kernel, len(sources), start, m_pad),
        in_specs=[pl.BlockSpec(memory_space=pltpu.SMEM), vmem, vmem]
        + [pl.BlockSpec(memory_space=pl.ANY)] * len(sources),
        out_specs=[vmem] * ranks,
        out_shape=[pltpu.VMEM(shape.shape, F32)] + [shape] * (ranks - 1),
        scratch_shapes=[
            pltpu.VMEM((columns, k_pad, scens, LANES), F32),
            pltpu.VMEM((scens, HALF, width), BF16),
            pltpu.SemaphoreType.DMA((len(sources), columns)),
        ],
        compiler_params=pltpu.CompilerParams(vmem_limit_bytes=VMEM_BYTES),
        cost_estimate=SMALL,
        name="wave",
    )(rank, *tables, *sources)


def level_kernel(
    step,
    rank_ref,
    count_ref,
    bus_hbm,
    cond_hbm,
    sat_hbm,
    volt_hbm,
    inject_hbm,
    there_ref,
    back_ref,
    zinv_ref,
    base_ref,
    sat_out,
    there_out,
    back_out,
    zinv_out,
    bus_ref,
    cond_ref,
    sat_ref,
    volt_ref,
    inject_ref,
    sems,
):
    pairs = [
        (bus_hbm, bus_ref),
        (cond_hbm, cond_ref),
        (sat_hbm, sat_ref),
        (volt_hbm, volt_ref),
        (inject_hbm, inject_ref),
        (there_ref.at[rank_ref[0]], there_out),
        (back_ref.at[rank_ref[0]], back_out),
        (zinv_ref, zinv_out),
    ]
    copies = [
        pltpu.make_async_copy(*pair, sems.at[q]) for q, pair in enumerate(pairs)
    ]
    for copy in copies:
        copy.start()
    for copy in copies[:3]:
        copy.wait()
    slots = bus_ref.shape[1]
    buses = volt_ref.shape[-1]
    total = jnp.zeros((16, buses), F32)
    for start in range(0, slots, step):
        at = pl.ds(start, step)
        slot_ids = lax.broadcasted_iota(jnp.int32, (1, step), 1) + start
        live = slot_ids < count_ref[0]
        pieces = []
        for ref in (cond_ref, sat_ref):
            rest = jnp.where(live, ref[:, at], 0.0)
            for _ in range(3):
                high = rest.astype(BF16).astype(F32)
                pieces.append(high)
                rest = rest - high
        pieces.append(jnp.zeros((10, step), F32))
        weights = jnp.concatenate(pieces, axis=0).astype(BF16)
        bus_ids = lax.broadcasted_iota(jnp.int32, (buses, step), 0)
        onehot = jnp.where(bus_ids == bus_ref[:, at], 1.0, 0.0).astype(BF16)
        total += lax.dot_general(
            weights, onehot, NT_DIMS, preferred_element_type=F32
        )
    cond = total[0:1] + total[1:2] + total[2:3]
    sat = total[3:4] + total[4:5] + total[5:6]
    sat_out[...] = jnp.broadcast_to(sat, sat_out.shape)
    for copy in copies[3:5]:
        copy.wait()
    for row in range(volt_ref.shape[0]):
        base_ref[row] = inject_ref[row] + cond * volt_ref[row]
    for copy in copies[5:]:
        copy.wait()


def levels(rank, dev_count, dev_bus, dev_cond, dev_sat, volt, inject, tables, zinv):
    slots = dev_bus.shape[1]
    buses = volt.shape[-1]
    step = 512 if slots % 512 == 0 else slots
    vmem = pl.BlockSpec(memory_space=pltpu.VMEM)
    smem = pl.BlockSpec(memory_space=pltpu.SMEM)
    anywhere = pl.BlockSpec(memory_space=pl.ANY)
    there, back = tables
    inputs = [
        pltpu.with_memory_space_constraint(each, pltpu.HBM)
        for each in (dev_bus, dev_cond, dev_sat, volt, inject, there, back)
    ] + [zinv]
    return pl.pallas_call(
        functools.partial(level_kernel, step),
        in_specs=[smem] * 2 + [anywhere] * len(inputs),
        out_specs=[vmem] * 5,
        out_shape=[
            pltpu.VMEM(volt.shape, F32),
            pltpu.VMEM((8, buses), F32),
            pltpu.VMEM(there.shape[1:], BF16),
            pltpu.VMEM(back.shape[1:], BF16),
            pltpu.VMEM(zinv.shape, BF16),
        ],
        scratch_shapes=[pltpu.VMEM(each.shape, each.dtype) for each in inputs[:5]]
        + [pltpu.SemaphoreType.DMA((len(inputs),))],
        compiler_params=pltpu.CompilerParams(vmem_limit_bytes=VMEM_BYTES),
        cost_estimate=SMALL,
        name="levels",
    )(rank, dev_count, *inputs)


def add_far(far, blocks, hot):
    for first in range(0, len(blocks), 2):
        parts = [split(block) for block in blocks[first : first + 2]]
        rows = slice(first * NBD, (first + len(parts)) * NBD)
        for piece in range(2):
            edges = jnp.concatenate([part[piece] for part in parts], axis=1)
            far += jnp.dot(edges, hot[rows], preferred_element_type=F32)
    return far


def tie_kernel(
    h_local, areas, origins, late_count, place_ref, *refs
):
    lists, refs = refs[:5], refs[5:]
    early = len(origins) - late_count
    blocks, refs = refs[:early], refs[early:]
    far_out, hot_out, adm_out, target_out = refs[:4]
    bus_ref, area_ref, far_ref, res_ref, reac_ref, held, sems = refs[4:]
    copies = [
        pltpu.make_async_copy(*pair, sems.at[q])
        for q, pair in enumerate(zip(lists, refs[4:9]))
    ]
    copies += [
        pltpu.make_async_copy(block, held.at[q], sems.at[5 + q])
        for q, block in enumerate(blocks)
    ]
    for copy in copies:
        copy.start()
    for copy in copies[:5]:
        copy.wait()
    ties = bus_ref.shape[1]
    edge_ids = lax.broadcasted_iota(jnp.int32, (NBD, ties), 0)
    far_hit = edge_ids == far_ref[...]
    hots = []
    for step, flip in origins:
        origin = (place_ref[1] + areas - step) % areas
        hit = area_ref[...] == (origin ^ 1 if flip else origin)
        hots.append(jnp.where(far_hit & hit, 1.0, 0.0).astype(BF16))
    hot_out[...] = jnp.concatenate(hots[early:], axis=0)
    target_out[...] = jnp.where(edge_ids == bus_ref[...], 1.0, 0.0).astype(BF16)
    resist = res_ref[...]
    for h in range(h_local):
        order = (2 * (place_ref[0] * h_local + h) + 1).astype(F32)
        reactance = reac_ref[...] * order
        denominator = resist * resist + reactance * reactance
        adm_out[pl.ds(h, 1), :] = resist / denominator
        adm_out[pl.ds(h_local + h, 1), :] = -reactance / denominator
    for copy in copies[5:]:
        copy.wait()
    far_out[...] = add_far(
        jnp.zeros(far_out.shape, F32),
        [held[q] for q in range(early)],
        jnp.concatenate(hots[:early], axis=0),
    )


def tie_parts(place, tie_lists, blocks, areas, origins, late_count, h_local):
    ties = tie_lists[0].shape[1]
    rows = blocks[0].shape[0]
    vmem = pl.BlockSpec(memory_space=pltpu.VMEM)
    return pl.pallas_call(
        functools.partial(tie_kernel, h_local, areas, origins, late_count),
        in_specs=[pl.BlockSpec(memory_space=pltpu.SMEM)]
        + [pl.BlockSpec(memory_space=pl.ANY)] * (len(tie_lists) + len(blocks)),
        out_specs=[vmem] * 4,
        out_shape=[
            pltpu.VMEM((rows, ties), F32),
            pltpu.VMEM((late_count * NBD, ties), BF16),
            pltpu.VMEM((2 * h_local, ties), F32),
            pltpu.VMEM((NBD, ties), BF16),
        ],
        scratch_shapes=[pltpu.VMEM(each.shape, each.dtype) for each in tie_lists]
        + [
            pltpu.VMEM((len(blocks), rows, NBD), F32),
            pltpu.SemaphoreType.DMA((len(blocks) + len(tie_lists),)),
        ],
        compiler_params=pltpu.CompilerParams(vmem_limit_bytes=VMEM_BYTES),
        cost_estimate=SMALL,
        name="ties",
    )(place, *tie_lists, *blocks)


def tie_currents(far, adm, target, scaled, h_local, scens):
    half = h_local * scens
    for h in range(h_local):
        adm_real, adm_imag = adm[h : h + 1], adm[h_local + h : h_local + h + 1]
        real = far[h * scens : (h + 1) * scens]
        imag = far[half + h * scens : half + (h + 1) * scens]
        scaled[pl.ds(h * scens, scens), :] = adm_real * real - adm_imag * imag
        scaled[pl.ds(half + h * scens, scens), :] = adm_real * imag + adm_imag * real
    high, low = split(scaled[...])
    return lax.dot_general(
        high, target, NT_DIMS, preferred_element_type=F32
    ) + lax.dot_general(low, target, NT_DIMS, preferred_element_type=F32)


def solve_kernel(start, width, ranks, late_count, place_ref, *refs):
    refs = list(refs)

    def take(count):
        taken, refs[:count] = refs[:count], []
        return taken

    base_ref, sat_ref, zinv_ref, _ = take(4)
    shaped_refs = take(ranks)
    last = late_count > 0
    if last:
        total_ref, far_ref, hot_ref, adm_ref, target_ref = take(5)
        blocks = take(late_count)
        out_ref, full, stage, sem, scaled, held, block_sems = refs
        block_copies = [
            pltpu.make_async_copy(block, held.at[q], block_sems.at[q])
            for q, block in enumerate(blocks)
        ]
        for copy in block_copies:
            copy.start()
    else:
        out_ref, mark_ref, full = refs
        mark_ref[...] = jnp.zeros(mark_ref.shape, F32)
        stage = out_ref
    _, h_local, scens, _ = base_ref.shape
    columns = shaped_refs[0].shape[0]
    part = scens // ranks
    for k, ref in enumerate(shaped_refs):
        quarter = pl.ds(pl.multiple_of((place_ref[0] ^ k) * part, 8), part)
        for j in range(columns):
            at = pl.ds(j * LANES, LANES)
            for row in range(2 * h_local):
                full[row, quarter, at] = ref[j, pl.ds(row * part, part), :]
    if last:
        for copy in block_copies:
            copy.wait()
        far = add_far(
            far_ref[...], [held[q] for q in range(late_count)], hot_ref[...]
        )
        ties = tie_currents(
            far, adm_ref[...], target_ref[...], scaled, h_local, scens
        )
    lanes = pl.ds(start, width)
    sat = sat_ref[0:1, lanes]
    copies = []
    for h in range(h_local):
        parts = []
        for c in range(2):
            row = c * h_local + h
            rhs = base_ref[c, h, :, lanes] + sat * full[row]
            if last:
                here = ties[row * scens : (row + 1) * scens]
                if width > NBD:
                    rhs = jnp.concatenate([rhs[:, :NBD] + here, rhs[:, NBD:]], axis=1)
                else:
                    rhs = rhs + here
            parts.append(rhs.astype(BF16))
        both = jnp.concatenate(parts, axis=0)
        by_real = lax.dot_general(
            both, zinv_ref[0, h, :, lanes], NT_DIMS, preferred_element_type=F32
        )
        by_imag = lax.dot_general(
            both, zinv_ref[1, h, :, lanes], NT_DIMS, preferred_element_type=F32
        )
        real = by_real[:scens] - by_imag[scens:]
        imag = by_real[scens:] + by_imag[:scens]
        if last:
            real = real + total_ref[0, h]
            imag = imag + total_ref[1, h]
        stage[0, h] = real
        stage[1, h] = imag
        if last:
            copy = pltpu.make_async_copy(stage.at[:, h], out_ref.at[:, h], sem.at[h])
            copy.start()
            copies.append(copy)
    for copy in copies:
        copy.wait()


def solve(place, base, sat, zinvs, shaped, tie, start, width):
    _, h_local, scens, _ = base.shape
    ranks = len(shaped)
    vmem = pl.BlockSpec(memory_space=pltpu.VMEM)
    anywhere = pl.BlockSpec(memory_space=pl.ANY)
    operands = [base, sat, *zinvs, *shaped]
    in_specs = [vmem] * len(operands)
    scratch = [pltpu.VMEM((2 * h_local, scens, width), F32)]
    late = []
    if tie is not None:
        total, parts, late = tie
        rows, ties = parts[0].shape
        operands += [total, *parts, *late]
        in_specs += [vmem] * (1 + len(parts)) + [anywhere] * len(late)
        out_specs = anywhere
        out_shape = jax.ShapeDtypeStruct(base.shape, F32)
        scratch += [
            pltpu.VMEM(base.shape, F32),
            pltpu.SemaphoreType.DMA((h_local,)),
            pltpu.VMEM((rows, ties), F32),
            pltpu.VMEM((len(late), rows, NBD), F32),
            pltpu.SemaphoreType.DMA((len(late),)),
        ]
    else:
        in_specs[3] = anywhere
        out_specs = [vmem, vmem]
        out_shape = [
            pltpu.VMEM(base.shape, F32),
            pltpu.VMEM((8, LANES), F32),
        ]
    return pl.pallas_call(
        functools.partial(solve_kernel, start, width, ranks, len(late)),
        in_specs=[pl.BlockSpec(memory_space=pltpu.SMEM)] + in_specs,
        out_specs=out_specs,
        out_shape=out_shape,
        scratch_shapes=scratch,
        compiler_params=pltpu.CompilerParams(vmem_limit_bytes=VMEM_BYTES),
        cost_estimate=SMALL,
        name="solve",
    )(place, *operands)


def per_device(
    volt,
    inject,
    zinv,
    dev_bus,
    dev_count,
    dev_cond,
    dev_sat,
    tie_bus,
    tie_area,
    tie_far,
    tie_res,
    tie_reac,
):
    _, _, h_local, scens, buses = volt.shape
    ranks = lax.axis_size("harm")
    areas = lax.axis_size("area")
    rank = lax.axis_index("harm")
    area = lax.axis_index("area")
    part = scens // ranks
    rows = 2 * h_local
    place = jnp.stack([rank, area]).astype(jnp.int32)
    there, back, _, m_pad = wave_tables(ranks, h_local)
    zinv = pltpu.with_memory_space_constraint(zinv[:, 0], pltpu.HBM)
    flat = volt.reshape(rows, scens, buses)

    def swap(value, k):
        return lax.ppermute(value, "harm", [(i, i ^ k) for i in range(ranks)])

    sizes = chunk_sizes(buses)
    starts = [buses - sum(sizes[: i + 1]) for i in range(len(sizes))]

    def piece(k):
        at = (0, (rank ^ k) * part, 0)
        return lax.dynamic_slice(flat, at, (rows, part, buses))

    pieces = [piece(k) for k in range(ranks - 1, 1, -1)]
    flat_now, *pieces = lax.optimization_barrier((flat, *pieces))
    far = [swap(each, ranks - 1 - q) for q, each in enumerate(pieces)]
    sibling = swap(flat_now, 1)
    sources = [flat, sibling] + far[::-1]

    edge = volt[..., :NBD].reshape(rows * scens, NBD)

    def shift(value, step):
        return lax.ppermute(
            value, "area", [(a, (a + step) % areas) for a in range(areas)]
        )

    def exchange(value):
        return lax.ppermute(value, "area", [(a, a ^ 1) for a in range(areas)])

    edge = after(edge, *pieces)
    blocks = [edge, exchange(edge)]
    base, sat, there, back, held = levels(
        place,
        dev_count,
        after(dev_bus, sibling),
        dev_cond,
        dev_sat,
        flat,
        inject.reshape(flat.shape),
        (jnp.asarray(there), jnp.asarray(back)),
        zinv,
    )
    def run_wave(index):
        return wave(
            place,
            (there, back),
            m_pad,
            sources,
            part,
            starts[index],
            sizes[index],
        )

    waves = [list(run_wave(index)) for index in range(len(sizes))]
    ring = {2: shift(edge, 2)}
    if areas > 4:
        ring[areas - 2] = shift(edge, areas - 2)
    for step in range(4, areas - 2, 2):
        ring[step] = shift(after(ring[step - 2], sat), 2)
    late = []
    origins, late_origins = [(0, 0), (0, 1)], []
    for step, block in ring.items():
        blocks.append(block)
        origins.append((step, 0))
        if step == 2:
            blocks.append(exchange(after(block, blocks[1], far[0], sat)))
            origins.append((step, 1))
        else:
            needs = blocks[3:4] if step == areas - 2 else [waves[-1][0]]
            late.append(exchange(after(block, *needs)))
            late_origins.append((step, 1))

    base = base.reshape(2, h_local, scens, buses)
    tie_lists = [
        pltpu.with_memory_space_constraint(each, pltpu.HBM)
        for each in (tie_bus, tie_area[:, :, 0], tie_far, tie_res, tie_reac)
    ]
    parts = tie_parts(
        place, tie_lists, blocks, areas, origins + late_origins, len(late), h_local
    )

    shaped = []
    for index, outs in enumerate(waves):
        if index == len(waves) - 1:
            outs[-1] = after(outs[-1], parts[0])
        shaped.append([outs[0]] + [swap(outs[k], k) for k in range(1, ranks)])
    total, mark = solve(
        place, base, sat, (held, zinv), shaped[0], None, starts[0], sizes[0]
    )
    total = solve(
        place,
        base,
        sat,
        (held, mark),
        shaped[1],
        (total, parts, late),
        starts[1],
        sizes[1],
    )
    return total[:, None]


def solution(mesh):
    wide = P(None, "area", "harm", None, None)
    flat = P("area", None)
    in_specs = (
        wide,
        wide,
        wide,
        flat,
        P("area"),
        flat,
        flat,
        flat,
        P("area", None, None),
        flat,
        flat,
        flat,
    )
    return jax.shard_map(
        per_device, mesh=mesh, in_specs=in_specs, out_specs=wide, check_vma=False
    )
```

```python
import functools

import jax
import jax.numpy as jnp
import numpy as np
from jax import lax
from jax.experimental import pallas as pl
from jax.experimental.pallas import tpu as pltpu
from jax.sharding import PartitionSpec as P

TS = 512
HALF = TS // 2
NBD = 128
LANES = 128
BF16 = jnp.bfloat16
F32 = jnp.float32
NT_DIMS = (((1,), (1,)), ((), ()))
VMEM_BYTES = 10 * 1024 * 1024
SMALL = pl.CostEstimate(flops=1000, bytes_accessed=1000, transcendentals=0)


def up(value, step):
    return -(-value // step) * step


def split(value):
    high = value.astype(BF16)
    return high, (value - high.astype(F32)).astype(BF16)


def np_split(value):
    value = np.asarray(value, np.float32)
    high = value.astype(jnp.bfloat16)
    return high, (value - high.astype(np.float32)).astype(jnp.bfloat16)


def chunk_sizes(buses):
    last = 256 if buses > 256 else buses
    return [buses - last, last] if buses > last else [last]


def after(value, *others):
    return lax.optimization_barrier((value, *others))[0] if others else value


def wave_tables(ranks, h_local):
    order_count = ranks * h_local
    samples = np.arange(HALF)[:, None]
    orders = 2 * np.arange(order_count)[None, :] + 1
    angles = (samples * orders % TS) * (2.0 * np.pi / TS)
    cos, sin = np.cos(angles), np.sin(angles)
    rows = 2 * h_local
    k_pad = up(ranks * rows, 16)
    m_pad = up(rows, 8)
    forward, inverse = [], []
    for rank in range(ranks):
        there = np.zeros((HALF, k_pad))
        back = np.zeros((ranks * m_pad, HALF))
        for k in range(ranks):
            own = slice((rank ^ k) * h_local, ((rank ^ k) + 1) * h_local)
            part = np.concatenate([cos[:, own], -sin[:, own]], axis=1)
            there[:, k * rows : (k + 1) * rows] = 2.0 * part
            back[k * m_pad : k * m_pad + rows] = (4.0 / TS) * part.T
        high, low = np_split(there)
        forward.append(np.concatenate([high, high, low], axis=1))
        high, low = np_split(back)
        inverse.append(np.concatenate([high, low], axis=0))
    return np.stack(forward), np.stack(inverse), k_pad, m_pad


def wave_kernel(source_count, start, m_pad, rank_ref, there_ref, back_ref, *refs):
    sources, outs = refs[:source_count], refs[source_count:-3]
    buf, shapes, sems = refs[-3:]
    ranks = len(outs)
    columns, k_pad, scens, _ = buf.shape
    rows = outs[0].shape[1] // scens
    mine = pl.ds(pl.multiple_of(rank_ref[0] * scens, 8), scens)
    copies = []
    used = 0
    for k, source in enumerate(sources):
        into = pl.ds(used, source.shape[0])
        used += source.shape[0]
        for j in range(columns):
            rows_at = mine if source.shape[1] > scens else pl.ds(0, scens)
            part = source.at[:, rows_at, pl.ds(start + j * LANES, LANES)]
            copy = pltpu.make_async_copy(part, buf.at[j, into], sems.at[k, j])
            copy.start()
            copies.append(copy)
    if k_pad > used:
        buf[:, pl.ds(used, k_pad - used)] = jnp.zeros(
            (columns, k_pad - used, scens, LANES), F32
        )
    for copy in copies:
        copy.wait()
    flat = buf.reshape(columns, k_pad * scens, LANES)
    for s in range(scens):
        volts = [flat[j, pl.ds(s, k_pad, stride=scens), :] for j in range(columns)]
        high, low = split(jnp.concatenate(volts, axis=1))
        stacked = jnp.concatenate([high, low, high], axis=0)
        wave = jnp.dot(there_ref[...], stacked, preferred_element_type=F32)
        shapes[s] = jnp.tanh(wave.astype(BF16))
    for s in range(scens):
        out = jnp.dot(back_ref[...], shapes[s], preferred_element_type=F32)
        out = out[: ranks * m_pad] + out[ranks * m_pad :]
        for k in range(ranks):
            for j in range(columns):
                outs[k][j, pl.ds(s, rows, stride=scens), :] = out[
                    k * m_pad : k * m_pad + rows, j * LANES : (j + 1) * LANES
                ]


def wave(rank, tables, m_pad, sources, scens, start, width):
    rows = sources[0].shape[0]
    ranks = sum(source.shape[0] for source in sources) // rows
    columns = width // LANES
    k_pad = tables[0].shape[1] // 3
    vmem = pl.BlockSpec(memory_space=pltpu.VMEM)
    shape = jax.ShapeDtypeStruct((columns, rows * scens, LANES), F32)
    return pl.pallas_call(
        functools.partial(wave_kernel, len(sources), start, m_pad),
        in_specs=[pl.BlockSpec(memory_space=pltpu.SMEM), vmem, vmem]
        + [pl.BlockSpec(memory_space=pl.ANY)] * len(sources),
        out_specs=[vmem] * ranks,
        out_shape=[pltpu.VMEM(shape.shape, F32)] + [shape] * (ranks - 1),
        scratch_shapes=[
            pltpu.VMEM((columns, k_pad, scens, LANES), F32),
            pltpu.VMEM((scens, HALF, width), BF16),
            pltpu.SemaphoreType.DMA((len(sources), columns)),
        ],
        compiler_params=pltpu.CompilerParams(vmem_limit_bytes=VMEM_BYTES),
        cost_estimate=SMALL,
        name="wave",
    )(rank, *tables, *sources)


def level_kernel(
    step,
    rank_ref,
    count_ref,
    bus_hbm,
    cond_hbm,
    sat_hbm,
    volt_hbm,
    inject_hbm,
    there_ref,
    back_ref,
    zinv_ref,
    base_ref,
    sat_out,
    there_out,
    back_out,
    zinv_out,
    bus_ref,
    cond_ref,
    sat_ref,
    volt_ref,
    inject_ref,
    sems,
):
    pairs = [
        (bus_hbm, bus_ref),
        (cond_hbm, cond_ref),
        (sat_hbm, sat_ref),
        (volt_hbm, volt_ref),
        (inject_hbm, inject_ref),
        (there_ref.at[rank_ref[0]], there_out),
        (back_ref.at[rank_ref[0]], back_out),
        (zinv_ref, zinv_out),
    ]
    copies = [
        pltpu.make_async_copy(*pair, sems.at[q]) for q, pair in enumerate(pairs)
    ]
    for copy in copies:
        copy.start()
    for copy in copies[:3]:
        copy.wait()
    slots = bus_ref.shape[1]
    buses = volt_ref.shape[-1]
    total = jnp.zeros((16, buses), F32)
    for start in range(0, slots, step):
        at = pl.ds(start, step)
        slot_ids = lax.broadcasted_iota(jnp.int32, (1, step), 1) + start
        live = slot_ids < count_ref[0]
        pieces = []
        for ref in (cond_ref, sat_ref):
            rest = jnp.where(live, ref[:, at], 0.0)
            for _ in range(3):
                high = rest.astype(BF16).astype(F32)
                pieces.append(high)
                rest = rest - high
        pieces.append(jnp.zeros((10, step), F32))
        weights = jnp.concatenate(pieces, axis=0).astype(BF16)
        bus_ids = lax.broadcasted_iota(jnp.int32, (buses, step), 0)
        onehot = jnp.where(bus_ids == bus_ref[:, at], 1.0, 0.0).astype(BF16)
        total += lax.dot_general(
            weights, onehot, NT_DIMS, preferred_element_type=F32
        )
    cond = total[0:1] + total[1:2] + total[2:3]
    sat = total[3:4] + total[4:5] + total[5:6]
    sat_out[...] = jnp.broadcast_to(sat, sat_out.shape)
    for copy in copies[3:5]:
        copy.wait()
    for row in range(volt_ref.shape[0]):
        base_ref[row] = inject_ref[row] + cond * volt_ref[row]
    for copy in copies[5:]:
        copy.wait()


def levels(rank, dev_count, dev_bus, dev_cond, dev_sat, volt, inject, tables, zinv):
    slots = dev_bus.shape[1]
    buses = volt.shape[-1]
    step = 512 if slots % 512 == 0 else slots
    vmem = pl.BlockSpec(memory_space=pltpu.VMEM)
    smem = pl.BlockSpec(memory_space=pltpu.SMEM)
    anywhere = pl.BlockSpec(memory_space=pl.ANY)
    there, back = tables
    inputs = [
        pltpu.with_memory_space_constraint(each, pltpu.HBM)
        for each in (dev_bus, dev_cond, dev_sat, volt, inject, there, back)
    ] + [zinv]
    return pl.pallas_call(
        functools.partial(level_kernel, step),
        in_specs=[smem] * 2 + [anywhere] * len(inputs),
        out_specs=[vmem] * 5,
        out_shape=[
            pltpu.VMEM(volt.shape, F32),
            pltpu.VMEM((8, buses), F32),
            pltpu.VMEM(there.shape[1:], BF16),
            pltpu.VMEM(back.shape[1:], BF16),
            pltpu.VMEM(zinv.shape, BF16),
        ],
        scratch_shapes=[pltpu.VMEM(each.shape, each.dtype) for each in inputs[:5]]
        + [pltpu.SemaphoreType.DMA((len(inputs),))],
        compiler_params=pltpu.CompilerParams(vmem_limit_bytes=VMEM_BYTES),
        cost_estimate=SMALL,
        name="levels",
    )(rank, dev_count, *inputs)


def add_far(far, blocks, hot):
    for first in range(0, len(blocks), 2):
        parts = [split(block) for block in blocks[first : first + 2]]
        rows = slice(first * NBD, (first + len(parts)) * NBD)
        for piece in range(2):
            edges = jnp.concatenate([part[piece] for part in parts], axis=1)
            far += jnp.dot(edges, hot[rows], preferred_element_type=F32)
    return far


def tie_kernel(
    h_local, areas, origins, late_count, place_ref, *refs
):
    lists, refs = refs[:5], refs[5:]
    early = len(origins) - late_count
    blocks, refs = refs[:early], refs[early:]
    far_out, hot_out, adm_out, target_out = refs[:4]
    bus_ref, area_ref, far_ref, res_ref, reac_ref, held, sems = refs[4:]
    copies = [
        pltpu.make_async_copy(*pair, sems.at[q])
        for q, pair in enumerate(zip(lists, refs[4:9]))
    ]
    copies += [
        pltpu.make_async_copy(block, held.at[q], sems.at[5 + q])
        for q, block in enumerate(blocks)
    ]
    for copy in copies:
        copy.start()
    for copy in copies[:5]:
        copy.wait()
    ties = bus_ref.shape[1]
    edge_ids = lax.broadcasted_iota(jnp.int32, (NBD, ties), 0)
    far_hit = edge_ids == far_ref[...]
    hots = []
    for step, flip in origins:
        origin = (place_ref[1] + areas - step) % areas
        hit = area_ref[...] == (origin ^ 1 if flip else origin)
        hots.append(jnp.where(far_hit & hit, 1.0, 0.0).astype(BF16))
    hot_out[...] = jnp.concatenate(hots[early:], axis=0)
    target_out[...] = jnp.where(edge_ids == bus_ref[...], 1.0, 0.0).astype(BF16)
    resist = res_ref[...]
    for h in range(h_local):
        order = (2 * (place_ref[0] * h_local + h) + 1).astype(F32)
        reactance = reac_ref[...] * order
        denominator = resist * resist + reactance * reactance
        adm_out[pl.ds(h, 1), :] = resist / denominator
        adm_out[pl.ds(h_local + h, 1), :] = -reactance / denominator
    for copy in copies[5:]:
        copy.wait()
    far_out[...] = add_far(
        jnp.zeros(far_out.shape, F32),
        [held[q] for q in range(early)],
        jnp.concatenate(hots[:early], axis=0),
    )


def tie_parts(place, tie_lists, blocks, areas, origins, late_count, h_local):
    ties = tie_lists[0].shape[1]
    rows = blocks[0].shape[0]
    vmem = pl.BlockSpec(memory_space=pltpu.VMEM)
    return pl.pallas_call(
        functools.partial(tie_kernel, h_local, areas, origins, late_count),
        in_specs=[pl.BlockSpec(memory_space=pltpu.SMEM)]
        + [pl.BlockSpec(memory_space=pl.ANY)] * (len(tie_lists) + len(blocks)),
        out_specs=[vmem] * 4,
        out_shape=[
            pltpu.VMEM((rows, ties), F32),
            pltpu.VMEM((late_count * NBD, ties), BF16),
            pltpu.VMEM((2 * h_local, ties), F32),
            pltpu.VMEM((NBD, ties), BF16),
        ],
        scratch_shapes=[pltpu.VMEM(each.shape, each.dtype) for each in tie_lists]
        + [
            pltpu.VMEM((len(blocks), rows, NBD), F32),
            pltpu.SemaphoreType.DMA((len(blocks) + len(tie_lists),)),
        ],
        compiler_params=pltpu.CompilerParams(vmem_limit_bytes=VMEM_BYTES),
        cost_estimate=SMALL,
        name="ties",
    )(place, *tie_lists, *blocks)


def tie_currents(far, adm, target, scaled, h_local, scens):
    half = h_local * scens
    for h in range(h_local):
        adm_real, adm_imag = adm[h : h + 1], adm[h_local + h : h_local + h + 1]
        real = far[h * scens : (h + 1) * scens]
        imag = far[half + h * scens : half + (h + 1) * scens]
        scaled[pl.ds(h * scens, scens), :] = adm_real * real - adm_imag * imag
        scaled[pl.ds(half + h * scens, scens), :] = adm_real * imag + adm_imag * real
    high, low = split(scaled[...])
    return lax.dot_general(
        high, target, NT_DIMS, preferred_element_type=F32
    ) + lax.dot_general(low, target, NT_DIMS, preferred_element_type=F32)


def solve_kernel(start, width, ranks, late_count, place_ref, *refs):
    refs = list(refs)

    def take(count):
        taken, refs[:count] = refs[:count], []
        return taken

    base_ref, sat_ref, zinv_ref, _ = take(4)
    shaped_refs = take(ranks)
    last = late_count > 0
    if last:
        total_ref, far_ref, hot_ref, adm_ref, target_ref = take(5)
        blocks = take(late_count)
        out_ref, full, stage, sem, scaled = refs
    else:
        out_ref, mark_ref, full = refs
        mark_ref[...] = jnp.zeros(mark_ref.shape, F32)
        stage = out_ref
    _, h_local, scens, _ = base_ref.shape
    columns = shaped_refs[0].shape[0]
    part = scens // ranks
    for k, ref in enumerate(shaped_refs):
        quarter = pl.ds(pl.multiple_of((place_ref[0] ^ k) * part, 8), part)
        for j in range(columns):
            at = pl.ds(j * LANES, LANES)
            for row in range(2 * h_local):
                full[row, quarter, at] = ref[j, pl.ds(row * part, part), :]
    if last:
        far = add_far(far_ref[...], [block[...] for block in blocks], hot_ref[...])
        ties = tie_currents(
            far, adm_ref[...], target_ref[...], scaled, h_local, scens
        )
    lanes = pl.ds(start, width)
    sat = sat_ref[0:1, lanes]
    copies = []
    for h in range(h_local):
        parts = []
        for c in range(2):
            row = c * h_local + h
            rhs = base_ref[c, h, :, lanes] + sat * full[row]
            if last:
                here = ties[row * scens : (row + 1) * scens]
                if width > NBD:
                    rhs = jnp.concatenate([rhs[:, :NBD] + here, rhs[:, NBD:]], axis=1)
                else:
                    rhs = rhs + here
            parts.append(rhs.astype(BF16))
        both = jnp.concatenate(parts, axis=0)
        by_real = lax.dot_general(
            both, zinv_ref[0, h, :, lanes], NT_DIMS, preferred_element_type=F32
        )
        by_imag = lax.dot_general(
            both, zinv_ref[1, h, :, lanes], NT_DIMS, preferred_element_type=F32
        )
        real = by_real[:scens] - by_imag[scens:]
        imag = by_real[scens:] + by_imag[:scens]
        if last:
            real = real + total_ref[0, h]
            imag = imag + total_ref[1, h]
        stage[0, h] = real
        stage[1, h] = imag
        if last:
            copy = pltpu.make_async_copy(stage.at[:, h], out_ref.at[:, h], sem.at[h])
            copy.start()
            copies.append(copy)
    for copy in copies:
        copy.wait()


def solve(place, base, sat, zinvs, shaped, tie, start, width):
    _, h_local, scens, _ = base.shape
    ranks = len(shaped)
    vmem = pl.BlockSpec(memory_space=pltpu.VMEM)
    anywhere = pl.BlockSpec(memory_space=pl.ANY)
    operands = [base, sat, *zinvs, *shaped]
    in_specs = [vmem] * len(operands)
    scratch = [pltpu.VMEM((2 * h_local, scens, width), F32)]
    late = []
    if tie is not None:
        total, parts, late = tie
        rows, ties = parts[0].shape
        operands += [total, *parts, *late]
        in_specs += [vmem] * (1 + len(parts) + len(late))
        out_specs = anywhere
        out_shape = jax.ShapeDtypeStruct(base.shape, F32)
        scratch += [
            pltpu.VMEM(base.shape, F32),
            pltpu.SemaphoreType.DMA((h_local,)),
            pltpu.VMEM((rows, ties), F32),
        ]
    else:
        in_specs[3] = anywhere
        out_specs = [vmem, vmem]
        out_shape = [
            pltpu.VMEM(base.shape, F32),
            pltpu.VMEM((8, LANES), F32),
        ]
    return pl.pallas_call(
        functools.partial(solve_kernel, start, width, ranks, len(late)),
        in_specs=[pl.BlockSpec(memory_space=pltpu.SMEM)] + in_specs,
        out_specs=out_specs,
        out_shape=out_shape,
        scratch_shapes=scratch,
        compiler_params=pltpu.CompilerParams(vmem_limit_bytes=VMEM_BYTES),
        cost_estimate=SMALL,
        name="solve",
    )(place, *operands)


def per_device(
    volt,
    inject,
    zinv,
    dev_bus,
    dev_count,
    dev_cond,
    dev_sat,
    tie_bus,
    tie_area,
    tie_far,
    tie_res,
    tie_reac,
):
    _, _, h_local, scens, buses = volt.shape
    ranks = lax.axis_size("harm")
    areas = lax.axis_size("area")
    rank = lax.axis_index("harm")
    area = lax.axis_index("area")
    part = scens // ranks
    rows = 2 * h_local
    place = jnp.stack([rank, area]).astype(jnp.int32)
    there, back, _, m_pad = wave_tables(ranks, h_local)
    zinv = pltpu.with_memory_space_constraint(zinv[:, 0], pltpu.HBM)
    flat = volt.reshape(rows, scens, buses)

    def swap(value, k):
        return lax.ppermute(value, "harm", [(i, i ^ k) for i in range(ranks)])

    sizes = chunk_sizes(buses)
    starts = [buses - sum(sizes[: i + 1]) for i in range(len(sizes))]

    def piece(k):
        at = (0, (rank ^ k) * part, 0)
        return lax.dynamic_slice(flat, at, (rows, part, buses))

    pieces = [piece(k) for k in range(ranks - 1, 1, -1)]
    flat_now, *pieces = lax.optimization_barrier((flat, *pieces))
    far = [swap(each, ranks - 1 - q) for q, each in enumerate(pieces)]
    sibling = swap(flat_now, 1)
    sources = [flat, sibling] + far[::-1]

    edge = volt[..., :NBD].reshape(rows * scens, NBD)

    def shift(value, step):
        return lax.ppermute(
            value, "area", [(a, (a + step) % areas) for a in range(areas)]
        )

    def exchange(value):
        return lax.ppermute(value, "area", [(a, a ^ 1) for a in range(areas)])

    edge = after(edge, *pieces)
    blocks = [edge, exchange(edge)]
    base, sat, there, back, held = levels(
        place,
        dev_count,
        after(dev_bus, sibling),
        dev_cond,
        dev_sat,
        flat,
        inject.reshape(flat.shape),
        (jnp.asarray(there), jnp.asarray(back)),
        zinv,
    )
    def run_wave(index):
        return wave(
            place,
            (there, back),
            m_pad,
            sources,
            part,
            starts[index],
            sizes[index],
        )

    waves = [list(run_wave(index)) for index in range(len(sizes))]
    ring = {2: shift(edge, 2)}
    if areas > 4:
        ring[areas - 2] = shift(edge, areas - 2)
    for step in range(4, areas - 2, 2):
        ring[step] = shift(after(ring[step - 2], ring[areas - 2], sat), 2)
    late = []
    origins, late_origins = [(0, 0), (0, 1)], []
    for step, block in ring.items():
        blocks.append(block)
        origins.append((step, 0))
        if step == 2:
            blocks.append(exchange(after(block, blocks[1], far[0], sat)))
            origins.append((step, 1))
        else:
            needs = blocks[3:4] if step == areas - 2 else [waves[-1][0]]
            late.append(exchange(after(block, *needs)))
            late_origins.append((step, 1))

    base = base.reshape(2, h_local, scens, buses)
    tie_lists = [
        pltpu.with_memory_space_constraint(each, pltpu.HBM)
        for each in (tie_bus, tie_area[:, :, 0], tie_far, tie_res, tie_reac)
    ]
    parts = tie_parts(
        place, tie_lists, blocks, areas, origins + late_origins, len(late), h_local
    )

    shaped = []
    for index, outs in enumerate(waves):
        got = [outs[0]] + [swap(outs[k], k) for k in range(1, ranks - 1)]
        if index == len(waves) - 1:
            outs[-1] = after(outs[-1], parts[0], got[1])
        shaped.append(got + [swap(outs[-1], ranks - 1)])
    total, mark = solve(
        place, base, sat, (held, zinv), shaped[0], None, starts[0], sizes[0]
    )
    total = solve(
        place,
        base,
        sat,
        (held, mark),
        shaped[1],
        (total, parts, late),
        starts[1],
        sizes[1],
    )
    return total[:, None]


def solution(mesh):
    wide = P(None, "area", "harm", None, None)
    flat = P("area", None)
    in_specs = (
        wide,
        wide,
        wide,
        flat,
        P("area"),
        flat,
        flat,
        flat,
        P("area", None, None),
        flat,
        flat,
        flat,
    )
    return jax.shard_map(
        per_device, mesh=mesh, in_specs=in_specs, out_specs=wide, check_vma=False
    )
```

```python
import functools

import jax
import jax.numpy as jnp
import numpy as np
from jax import lax
from jax.experimental import pallas as pl
from jax.experimental.pallas import tpu as pltpu
from jax.sharding import PartitionSpec as P

TS = 512
HALF = TS // 2
NBD = 128
LANES = 128
BF16 = jnp.bfloat16
F32 = jnp.float32
NT_DIMS = (((1,), (1,)), ((), ()))
VMEM_BYTES = 10 * 1024 * 1024
SMALL = pl.CostEstimate(flops=1000, bytes_accessed=1000, transcendentals=0)


def up(value, step):
    return -(-value // step) * step


def split(value):
    high = value.astype(BF16)
    return high, (value - high.astype(F32)).astype(BF16)


def np_split(value):
    value = np.asarray(value, np.float32)
    high = value.astype(jnp.bfloat16)
    return high, (value - high.astype(np.float32)).astype(jnp.bfloat16)


def chunk_sizes(buses):
    last = 256 if buses > 256 else buses
    return [buses - last, last] if buses > last else [last]


def after(value, *others):
    return lax.optimization_barrier((value, *others))[0] if others else value


def wave_tables(ranks, h_local):
    order_count = ranks * h_local
    samples = np.arange(HALF)[:, None]
    orders = 2 * np.arange(order_count)[None, :] + 1
    angles = (samples * orders % TS) * (2.0 * np.pi / TS)
    cos, sin = np.cos(angles), np.sin(angles)
    rows = 2 * h_local
    k_pad = up(ranks * rows, 16)
    m_pad = up(rows, 8)
    forward, inverse = [], []
    for rank in range(ranks):
        there = np.zeros((HALF, k_pad))
        back = np.zeros((ranks * m_pad, HALF))
        for k in range(ranks):
            own = slice((rank ^ k) * h_local, ((rank ^ k) + 1) * h_local)
            part = np.concatenate([cos[:, own], -sin[:, own]], axis=1)
            there[:, k * rows : (k + 1) * rows] = 2.0 * part
            back[k * m_pad : k * m_pad + rows] = (4.0 / TS) * part.T
        high, low = np_split(there)
        forward.append(np.concatenate([high, high, low], axis=1))
        high, low = np_split(back)
        inverse.append(np.concatenate([high, low], axis=0))
    return np.stack(forward), np.stack(inverse), k_pad, m_pad


def wave_kernel(source_count, start, m_pad, rank_ref, there_ref, back_ref, *refs):
    sources, outs = refs[:source_count], refs[source_count:-3]
    buf, shapes, sems = refs[-3:]
    ranks = len(outs)
    columns, k_pad, scens, _ = buf.shape
    rows = outs[0].shape[1] // scens
    mine = pl.ds(pl.multiple_of(rank_ref[0] * scens, 8), scens)
    copies = []
    used = 0
    for k, source in enumerate(sources):
        into = pl.ds(used, source.shape[0])
        used += source.shape[0]
        for j in range(columns):
            rows_at = mine if source.shape[1] > scens else pl.ds(0, scens)
            part = source.at[:, rows_at, pl.ds(start + j * LANES, LANES)]
            copy = pltpu.make_async_copy(part, buf.at[j, into], sems.at[k, j])
            copy.start()
            copies.append(copy)
    if k_pad > used:
        buf[:, pl.ds(used, k_pad - used)] = jnp.zeros(
            (columns, k_pad - used, scens, LANES), F32
        )
    for copy in copies:
        copy.wait()
    flat = buf.reshape(columns, k_pad * scens, LANES)
    for s in range(scens):
        volts = [flat[j, pl.ds(s, k_pad, stride=scens), :] for j in range(columns)]
        high, low = split(jnp.concatenate(volts, axis=1))
        stacked = jnp.concatenate([high, low, high], axis=0)
        wave = jnp.dot(there_ref[...], stacked, preferred_element_type=F32)
        shapes[s] = jnp.tanh(wave.astype(BF16))
    for s in range(scens):
        out = jnp.dot(back_ref[...], shapes[s], preferred_element_type=F32)
        out = out[: ranks * m_pad] + out[ranks * m_pad :]
        for k in range(ranks):
            for j in range(columns):
                outs[k][j, pl.ds(s, rows, stride=scens), :] = out[
                    k * m_pad : k * m_pad + rows, j * LANES : (j + 1) * LANES
                ]


def wave(rank, tables, m_pad, sources, scens, start, width):
    rows = sources[0].shape[0]
    ranks = sum(source.shape[0] for source in sources) // rows
    columns = width // LANES
    k_pad = tables[0].shape[1] // 3
    vmem = pl.BlockSpec(memory_space=pltpu.VMEM)
    shape = jax.ShapeDtypeStruct((columns, rows * scens, LANES), F32)
    return pl.pallas_call(
        functools.partial(wave_kernel, len(sources), start, m_pad),
        in_specs=[pl.BlockSpec(memory_space=pltpu.SMEM), vmem, vmem]
        + [pl.BlockSpec(memory_space=pl.ANY)] * len(sources),
        out_specs=[vmem] * ranks,
        out_shape=[pltpu.VMEM(shape.shape, F32)] + [shape] * (ranks - 1),
        scratch_shapes=[
            pltpu.VMEM((columns, k_pad, scens, LANES), F32),
            pltpu.VMEM((scens, HALF, width), BF16),
            pltpu.SemaphoreType.DMA((len(sources), columns)),
        ],
        compiler_params=pltpu.CompilerParams(vmem_limit_bytes=VMEM_BYTES),
        cost_estimate=SMALL,
        name="wave",
    )(rank, *tables, *sources)


def level_kernel(
    step,
    rank_ref,
    count_ref,
    bus_hbm,
    cond_hbm,
    sat_hbm,
    volt_hbm,
    inject_hbm,
    there_ref,
    back_ref,
    zinv_ref,
    base_ref,
    sat_out,
    there_out,
    back_out,
    zinv_out,
    turned_out,
    bus_ref,
    cond_ref,
    sat_ref,
    volt_ref,
    inject_ref,
    sems,
):
    pairs = [
        (bus_hbm, bus_ref),
        (cond_hbm, cond_ref),
        (sat_hbm, sat_ref),
        (volt_hbm, volt_ref),
        (inject_hbm, inject_ref),
        (there_ref.at[rank_ref[0]], there_out),
        (back_ref.at[rank_ref[0]], back_out),
    ]
    pairs += [
        (zinv_ref.at[c, h], zinv_out.at[c, h])
        for h in range(zinv_ref.shape[1])
        for c in range(2)
    ]
    copies = [
        pltpu.make_async_copy(*pair, sems.at[q]) for q, pair in enumerate(pairs)
    ]
    for copy in copies:
        copy.start()
    for copy in copies[:3]:
        copy.wait()
    slots = bus_ref.shape[1]
    buses = volt_ref.shape[-1]
    total = jnp.zeros((16, buses), F32)
    for start in range(0, slots, step):
        at = pl.ds(start, step)
        slot_ids = lax.broadcasted_iota(jnp.int32, (1, step), 1) + start
        live = slot_ids < count_ref[0]
        pieces = []
        for ref in (cond_ref, sat_ref):
            rest = jnp.where(live, ref[:, at], 0.0)
            for _ in range(3):
                high = rest.astype(BF16).astype(F32)
                pieces.append(high)
                rest = rest - high
        pieces.append(jnp.zeros((10, step), F32))
        weights = jnp.concatenate(pieces, axis=0).astype(BF16)
        bus_ids = lax.broadcasted_iota(jnp.int32, (buses, step), 0)
        onehot = jnp.where(bus_ids == bus_ref[:, at], 1.0, 0.0).astype(BF16)
        total += lax.dot_general(
            weights, onehot, NT_DIMS, preferred_element_type=F32
        )
    cond = total[0:1] + total[1:2] + total[2:3]
    sat = total[3:4] + total[4:5] + total[5:6]
    sat_out[...] = jnp.broadcast_to(sat, sat_out.shape)
    for copy in copies[3:5]:
        copy.wait()
    for row in range(volt_ref.shape[0]):
        base_ref[row] = inject_ref[row] + cond * volt_ref[row]
    for copy in copies[5:7]:
        copy.wait()
    turned = turned_out.shape[2]
    for q, copy in enumerate(copies[7:]):
        copy.wait()
        turned_out[q % 2, q // 2] = zinv_out[q % 2, q // 2, :, :turned].T


def levels(rank, dev_count, dev_bus, dev_cond, dev_sat, volt, inject, tables, zinv, turned):
    slots = dev_bus.shape[1]
    buses = volt.shape[-1]
    step = 512 if slots % 512 == 0 else slots
    vmem = pl.BlockSpec(memory_space=pltpu.VMEM)
    smem = pl.BlockSpec(memory_space=pltpu.SMEM)
    anywhere = pl.BlockSpec(memory_space=pl.ANY)
    there, back = tables
    inputs = [
        pltpu.with_memory_space_constraint(each, pltpu.HBM)
        for each in (dev_bus, dev_cond, dev_sat, volt, inject, there, back)
    ] + [zinv]
    return pl.pallas_call(
        functools.partial(level_kernel, step),
        in_specs=[smem] * 2 + [anywhere] * len(inputs),
        out_specs=[vmem] * 6,
        out_shape=[
            pltpu.VMEM(volt.shape, F32),
            pltpu.VMEM((8, buses), F32),
            pltpu.VMEM(there.shape[1:], BF16),
            pltpu.VMEM(back.shape[1:], BF16),
            pltpu.VMEM(zinv.shape, BF16),
            pltpu.VMEM(zinv.shape[:2] + (turned, buses), BF16),
        ],
        scratch_shapes=[pltpu.VMEM(each.shape, each.dtype) for each in inputs[:5]]
        + [pltpu.SemaphoreType.DMA((len(inputs) + 2 * zinv.shape[1],))],
        compiler_params=pltpu.CompilerParams(vmem_limit_bytes=VMEM_BYTES),
        cost_estimate=SMALL,
        name="levels",
    )(rank, dev_count, *inputs)


def add_far(far, blocks, hot):
    for first in range(0, len(blocks), 2):
        parts = [split(block) for block in blocks[first : first + 2]]
        rows = slice(first * NBD, (first + len(parts)) * NBD)
        for piece in range(2):
            edges = jnp.concatenate([part[piece] for part in parts], axis=1)
            far += jnp.dot(edges, hot[rows], preferred_element_type=F32)
    return far


def tie_kernel(
    h_local, areas, origins, late_count, place_ref, *refs
):
    lists, refs = refs[:5], refs[5:]
    early = len(origins) - late_count
    blocks, refs = refs[:early], refs[early:]
    far_out, hot_out, adm_out, target_out = refs[:4]
    bus_ref, area_ref, far_ref, res_ref, reac_ref, held, sems = refs[4:]
    copies = [
        pltpu.make_async_copy(*pair, sems.at[q])
        for q, pair in enumerate(zip(lists, refs[4:9]))
    ]
    copies += [
        pltpu.make_async_copy(block, held.at[q], sems.at[5 + q])
        for q, block in enumerate(blocks)
    ]
    for copy in copies:
        copy.start()
    for copy in copies[:5]:
        copy.wait()
    ties = bus_ref.shape[1]
    edge_ids = lax.broadcasted_iota(jnp.int32, (NBD, ties), 0)
    far_hit = edge_ids == far_ref[...]
    hots = []
    for step, flip in origins:
        origin = (place_ref[1] + areas - step) % areas
        hit = area_ref[...] == (origin ^ 1 if flip else origin)
        hots.append(jnp.where(far_hit & hit, 1.0, 0.0).astype(BF16))
    hot_out[...] = jnp.concatenate(hots[early:], axis=0)
    target_out[...] = jnp.where(edge_ids == bus_ref[...], 1.0, 0.0).astype(BF16)
    resist = res_ref[...]
    for h in range(h_local):
        order = (2 * (place_ref[0] * h_local + h) + 1).astype(F32)
        reactance = reac_ref[...] * order
        denominator = resist * resist + reactance * reactance
        adm_out[pl.ds(h, 1), :] = resist / denominator
        adm_out[pl.ds(h_local + h, 1), :] = -reactance / denominator
    for copy in copies[5:]:
        copy.wait()
    far_out[...] = add_far(
        jnp.zeros(far_out.shape, F32),
        [held[q] for q in range(early)],
        jnp.concatenate(hots[:early], axis=0),
    )


def tie_parts(place, tie_lists, blocks, areas, origins, late_count, h_local):
    ties = tie_lists[0].shape[1]
    rows = blocks[0].shape[0]
    vmem = pl.BlockSpec(memory_space=pltpu.VMEM)
    return pl.pallas_call(
        functools.partial(tie_kernel, h_local, areas, origins, late_count),
        in_specs=[pl.BlockSpec(memory_space=pltpu.SMEM)]
        + [pl.BlockSpec(memory_space=pl.ANY)] * (len(tie_lists) + len(blocks)),
        out_specs=[vmem] * 4,
        out_shape=[
            pltpu.VMEM((rows, ties), F32),
            pltpu.VMEM((late_count * NBD, ties), BF16),
            pltpu.VMEM((2 * h_local, ties), F32),
            pltpu.VMEM((NBD, ties), BF16),
        ],
        scratch_shapes=[pltpu.VMEM(each.shape, each.dtype) for each in tie_lists]
        + [
            pltpu.VMEM((len(blocks), rows, NBD), F32),
            pltpu.SemaphoreType.DMA((len(blocks) + len(tie_lists),)),
        ],
        compiler_params=pltpu.CompilerParams(vmem_limit_bytes=VMEM_BYTES),
        cost_estimate=SMALL,
        name="ties",
    )(place, *tie_lists, *blocks)


def tie_currents(far, adm, target, scaled, h_local, scens):
    half = h_local * scens
    for h in range(h_local):
        adm_real, adm_imag = adm[h : h + 1], adm[h_local + h : h_local + h + 1]
        real = far[h * scens : (h + 1) * scens]
        imag = far[half + h * scens : half + (h + 1) * scens]
        scaled[pl.ds(h * scens, scens), :] = adm_real * real - adm_imag * imag
        scaled[pl.ds(half + h * scens, scens), :] = adm_real * imag + adm_imag * real
    high, low = split(scaled[...])
    return lax.dot_general(
        high, target, NT_DIMS, preferred_element_type=F32
    ) + lax.dot_general(low, target, NT_DIMS, preferred_element_type=F32)


def solve_kernel(start, width, ranks, late_count, place_ref, *refs):
    refs = list(refs)

    def take(count):
        taken, refs[:count] = refs[:count], []
        return taken

    base_ref, sat_ref, zinv_ref, _ = take(4)
    shaped_refs = take(ranks)
    last = late_count > 0
    if last:
        total_ref, far_ref, hot_ref, adm_ref, target_ref = take(5)
        blocks = take(late_count)
        out_ref, full, stage, sem, scaled = refs
    else:
        out_ref, mark_ref, full = refs
        mark_ref[...] = jnp.zeros(mark_ref.shape, F32)
        stage = out_ref
    _, h_local, scens, _ = base_ref.shape
    columns = shaped_refs[0].shape[0]
    part = scens // ranks
    for k, ref in enumerate(shaped_refs):
        quarter = pl.ds(pl.multiple_of((place_ref[0] ^ k) * part, 8), part)
        for j in range(columns):
            at = pl.ds(j * LANES, LANES)
            for row in range(2 * h_local):
                full[row, quarter, at] = ref[j, pl.ds(row * part, part), :]
    if last:
        far = add_far(far_ref[...], [block[...] for block in blocks], hot_ref[...])
        ties = tie_currents(
            far, adm_ref[...], target_ref[...], scaled, h_local, scens
        )
    lanes = pl.ds(start, width)
    sat = sat_ref[0:1, lanes]
    copies = []
    for h in range(h_local):
        parts = []
        for c in range(2):
            row = c * h_local + h
            rhs = base_ref[c, h, :, lanes] + sat * full[row]
            if last:
                here = ties[row * scens : (row + 1) * scens]
                if width > NBD:
                    rhs = jnp.concatenate([rhs[:, :NBD] + here, rhs[:, NBD:]], axis=1)
                else:
                    rhs = rhs + here
            parts.append(rhs.astype(BF16))
        both = jnp.concatenate(parts, axis=0)
        if last:
            by_real = jnp.dot(both, zinv_ref[0, h], preferred_element_type=F32)
            by_imag = jnp.dot(both, zinv_ref[1, h], preferred_element_type=F32)
        else:
            by_real = lax.dot_general(
                both, zinv_ref[0, h, :, lanes], NT_DIMS, preferred_element_type=F32
            )
            by_imag = lax.dot_general(
                both, zinv_ref[1, h, :, lanes], NT_DIMS, preferred_element_type=F32
            )
        real = by_real[:scens] - by_imag[scens:]
        imag = by_real[scens:] + by_imag[:scens]
        if last:
            real = real + total_ref[0, h]
            imag = imag + total_ref[1, h]
        stage[0, h] = real
        stage[1, h] = imag
        if last:
            copy = pltpu.make_async_copy(stage.at[:, h], out_ref.at[:, h], sem.at[h])
            copy.start()
            copies.append(copy)
    for copy in copies:
        copy.wait()


def solve(place, base, sat, zinvs, shaped, tie, start, width):
    _, h_local, scens, _ = base.shape
    ranks = len(shaped)
    vmem = pl.BlockSpec(memory_space=pltpu.VMEM)
    anywhere = pl.BlockSpec(memory_space=pl.ANY)
    operands = [base, sat, *zinvs, *shaped]
    in_specs = [vmem] * len(operands)
    scratch = [pltpu.VMEM((2 * h_local, scens, width), F32)]
    late = []
    if tie is not None:
        total, parts, late = tie
        rows, ties = parts[0].shape
        operands += [total, *parts, *late]
        in_specs += [vmem] * (1 + len(parts) + len(late))
        out_specs = anywhere
        out_shape = jax.ShapeDtypeStruct(base.shape, F32)
        scratch += [
            pltpu.VMEM(base.shape, F32),
            pltpu.SemaphoreType.DMA((h_local,)),
            pltpu.VMEM((rows, ties), F32),
        ]
    else:
        in_specs[3] = anywhere
        out_specs = [vmem, vmem]
        out_shape = [
            pltpu.VMEM(base.shape, F32),
            pltpu.VMEM((8, LANES), F32),
        ]
    return pl.pallas_call(
        functools.partial(solve_kernel, start, width, ranks, len(late)),
        in_specs=[pl.BlockSpec(memory_space=pltpu.SMEM)] + in_specs,
        out_specs=out_specs,
        out_shape=out_shape,
        scratch_shapes=scratch,
        compiler_params=pltpu.CompilerParams(vmem_limit_bytes=VMEM_BYTES),
        cost_estimate=SMALL,
        name="solve",
    )(place, *operands)


def per_device(
    volt,
    inject,
    zinv,
    dev_bus,
    dev_count,
    dev_cond,
    dev_sat,
    tie_bus,
    tie_area,
    tie_far,
    tie_res,
    tie_reac,
):
    _, _, h_local, scens, buses = volt.shape
    ranks = lax.axis_size("harm")
    areas = lax.axis_size("area")
    rank = lax.axis_index("harm")
    area = lax.axis_index("area")
    part = scens // ranks
    rows = 2 * h_local
    place = jnp.stack([rank, area]).astype(jnp.int32)
    there, back, _, m_pad = wave_tables(ranks, h_local)
    zinv = pltpu.with_memory_space_constraint(zinv[:, 0], pltpu.HBM)
    flat = volt.reshape(rows, scens, buses)

    def swap(value, k):
        return lax.ppermute(value, "harm", [(i, i ^ k) for i in range(ranks)])

    sizes = chunk_sizes(buses)
    starts = [buses - sum(sizes[: i + 1]) for i in range(len(sizes))]

    def piece(k):
        at = (0, (rank ^ k) * part, 0)
        return lax.dynamic_slice(flat, at, (rows, part, buses))

    pieces = [piece(k) for k in range(ranks - 1, 1, -1)]
    flat_now, *pieces = lax.optimization_barrier((flat, *pieces))
    far = [swap(each, ranks - 1 - q) for q, each in enumerate(pieces)]
    sibling = swap(flat_now, 1)
    sources = [flat, sibling] + far[::-1]

    edge = volt[..., :NBD].reshape(rows * scens, NBD)

    def shift(value, step):
        return lax.ppermute(
            value, "area", [(a, (a + step) % areas) for a in range(areas)]
        )

    def exchange(value):
        return lax.ppermute(value, "area", [(a, a ^ 1) for a in range(areas)])

    edge = after(edge, *pieces)
    blocks = [edge, exchange(edge)]
    base, sat, there, back, held, turned = levels(
        place,
        dev_count,
        after(dev_bus, sibling),
        dev_cond,
        dev_sat,
        flat,
        inject.reshape(flat.shape),
        (jnp.asarray(there), jnp.asarray(back)),
        zinv,
        sizes[-1],
    )
    def run_wave(index):
        return wave(
            place,
            (there, back),
            m_pad,
            sources,
            part,
            starts[index],
            sizes[index],
        )

    waves = [list(run_wave(index)) for index in range(len(sizes))]
    ring = {2: shift(edge, 2)}
    if areas > 4:
        ring[areas - 2] = shift(edge, areas - 2)
    for step in range(4, areas - 2, 2):
        ring[step] = shift(after(ring[step - 2], ring[areas - 2], sat), 2)
    late = []
    origins, late_origins = [(0, 0), (0, 1)], []
    for step, block in ring.items():
        blocks.append(block)
        origins.append((step, 0))
        if step == 2:
            blocks.append(exchange(after(block, blocks[1], far[0], sat)))
            origins.append((step, 1))
        else:
            needs = blocks[3:4] if step == areas - 2 else [waves[-1][0]]
            late.append(exchange(after(block, *needs)))
            late_origins.append((step, 1))

    base = base.reshape(2, h_local, scens, buses)
    tie_lists = [
        pltpu.with_memory_space_constraint(each, pltpu.HBM)
        for each in (tie_bus, tie_area[:, :, 0], tie_far, tie_res, tie_reac)
    ]
    parts = tie_parts(
        place, tie_lists, blocks, areas, origins + late_origins, len(late), h_local
    )

    shaped = []
    for index, outs in enumerate(waves):
        got = [outs[0]] + [swap(outs[k], k) for k in range(1, ranks - 1)]
        if index == len(waves) - 1:
            outs[-1] = after(outs[-1], parts[0], got[1])
        shaped.append(got + [swap(outs[-1], ranks - 1)])
    total, mark = solve(
        place, base, sat, (held, zinv), shaped[0], None, starts[0], sizes[0]
    )
    total = solve(
        place,
        base,
        sat,
        (turned, mark),
        shaped[1],
        (total, parts, late),
        starts[1],
        sizes[1],
    )
    return total[:, None]


def solution(mesh):
    wide = P(None, "area", "harm", None, None)
    flat = P("area", None)
    in_specs = (
        wide,
        wide,
        wide,
        flat,
        P("area"),
        flat,
        flat,
        flat,
        P("area", None, None),
        flat,
        flat,
        flat,
    )
    return jax.shard_map(
        per_device, mesh=mesh, in_specs=in_specs, out_specs=wide, check_vma=False
    )
```

```python
import functools

import jax
import jax.numpy as jnp
import numpy as np
from jax import lax
from jax.experimental import pallas as pl
from jax.experimental.pallas import tpu as pltpu
from jax.sharding import PartitionSpec as P

TS = 512
HALF = TS // 2
NBD = 128
LANES = 128
BF16 = jnp.bfloat16
F32 = jnp.float32
NT_DIMS = (((1,), (1,)), ((), ()))
VMEM_BYTES = 10 * 1024 * 1024
SMALL = pl.CostEstimate(flops=1000, bytes_accessed=1000, transcendentals=0)


def up(value, step):
    return -(-value // step) * step


def split(value):
    high = value.astype(BF16)
    return high, (value - high.astype(F32)).astype(BF16)


def np_split(value):
    value = np.asarray(value, np.float32)
    high = value.astype(jnp.bfloat16)
    return high, (value - high.astype(np.float32)).astype(jnp.bfloat16)


def chunk_sizes(buses):
    last = 256 if buses > 256 else buses
    return [buses - last, last] if buses > last else [last]


def after(value, *others):
    return lax.optimization_barrier((value, *others))[0] if others else value


def wave_tables(ranks, h_local):
    order_count = ranks * h_local
    samples = np.arange(HALF)[:, None]
    orders = 2 * np.arange(order_count)[None, :] + 1
    angles = (samples * orders % TS) * (2.0 * np.pi / TS)
    cos, sin = np.cos(angles), np.sin(angles)
    rows = 2 * h_local
    k_pad = up(ranks * rows, 16)
    m_pad = up(rows, 8)
    forward, inverse = [], []
    for rank in range(ranks):
        there = np.zeros((HALF, k_pad))
        back = np.zeros((ranks * m_pad, HALF))
        for k in range(ranks):
            own = slice((rank ^ k) * h_local, ((rank ^ k) + 1) * h_local)
            part = np.concatenate([cos[:, own], -sin[:, own]], axis=1)
            there[:, k * rows : (k + 1) * rows] = 2.0 * part
            back[k * m_pad : k * m_pad + rows] = (4.0 / TS) * part.T
        high, low = np_split(there)
        forward.append(np.concatenate([high, high, low], axis=1))
        high, low = np_split(back)
        inverse.append(np.concatenate([high, low], axis=0))
    return np.stack(forward), np.stack(inverse), k_pad, m_pad


def piece_kernel(partners, place_ref, volt_ref, *refs):
    outs, sems = refs[:-1], refs[-1]
    copies = []
    for q, (out, k) in enumerate(zip(outs, partners)):
        part = out.shape[1]
        at = pl.ds(pl.multiple_of((place_ref[0] ^ k) * part, 8), part)
        copies.append(pltpu.make_async_copy(volt_ref.at[:, at], out, sems.at[q]))
    for copy in copies:
        copy.start()
    for copy in copies:
        copy.wait()


def send_pieces(place, volt, partners, part):
    shape = jax.ShapeDtypeStruct((volt.shape[0], part, volt.shape[2]), F32)
    vmem = pl.BlockSpec(memory_space=pltpu.VMEM)
    return pl.pallas_call(
        functools.partial(piece_kernel, partners),
        in_specs=[
            pl.BlockSpec(memory_space=pltpu.SMEM),
            pl.BlockSpec(memory_space=pl.ANY),
        ],
        out_specs=[vmem] * len(partners),
        out_shape=[pltpu.VMEM(shape.shape, F32)] * len(partners),
        scratch_shapes=[pltpu.SemaphoreType.DMA((len(partners),))],
        cost_estimate=SMALL,
        name="pieces",
    )(place, volt)


def wave_kernel(source_count, start, m_pad, rank_ref, there_ref, back_ref, *refs):
    sources, outs = refs[:source_count], refs[source_count:-3]
    buf, shapes, sems = refs[-3:]
    ranks = len(outs)
    columns, k_pad, scens, _ = buf.shape
    rows = outs[0].shape[1] // scens
    mine = pl.ds(pl.multiple_of(rank_ref[0] * scens, 8), scens)
    copies = []
    used = 0
    for k, source in enumerate(sources):
        into = pl.ds(used, source.shape[0])
        used += source.shape[0]
        for j in range(columns):
            rows_at = mine if source.shape[1] > scens else pl.ds(0, scens)
            part = source.at[:, rows_at, pl.ds(start + j * LANES, LANES)]
            copy = pltpu.make_async_copy(part, buf.at[j, into], sems.at[k, j])
            copy.start()
            copies.append(copy)
    if k_pad > used:
        buf[:, pl.ds(used, k_pad - used)] = jnp.zeros(
            (columns, k_pad - used, scens, LANES), F32
        )
    for copy in copies:
        copy.wait()
    flat = buf.reshape(columns, k_pad * scens, LANES)
    for s in range(scens):
        volts = [flat[j, pl.ds(s, k_pad, stride=scens), :] for j in range(columns)]
        high, low = split(jnp.concatenate(volts, axis=1))
        stacked = jnp.concatenate([high, low, high], axis=0)
        wave = jnp.dot(there_ref[...], stacked, preferred_element_type=F32)
        shapes[s] = jnp.tanh(wave.astype(BF16))
    for s in range(scens):
        out = jnp.dot(back_ref[...], shapes[s], preferred_element_type=F32)
        out = out[: ranks * m_pad] + out[ranks * m_pad :]
        for k in range(ranks):
            for j in range(columns):
                outs[k][j, pl.ds(s, rows, stride=scens), :] = out[
                    k * m_pad : k * m_pad + rows, j * LANES : (j + 1) * LANES
                ]


def wave(rank, tables, m_pad, sources, scens, start, width):
    rows = sources[0].shape[0]
    ranks = sum(source.shape[0] for source in sources) // rows
    columns = width // LANES
    k_pad = tables[0].shape[1] // 3
    vmem = pl.BlockSpec(memory_space=pltpu.VMEM)
    shape = jax.ShapeDtypeStruct((columns, rows * scens, LANES), F32)
    return pl.pallas_call(
        functools.partial(wave_kernel, len(sources), start, m_pad),
        in_specs=[pl.BlockSpec(memory_space=pltpu.SMEM), vmem, vmem]
        + [pl.BlockSpec(memory_space=pl.ANY)] * len(sources),
        out_specs=[vmem] * ranks,
        out_shape=[pltpu.VMEM(shape.shape, F32)] + [shape] * (ranks - 1),
        scratch_shapes=[
            pltpu.VMEM((columns, k_pad, scens, LANES), F32),
            pltpu.VMEM((scens, HALF, width), BF16),
            pltpu.SemaphoreType.DMA((len(sources), columns)),
        ],
        compiler_params=pltpu.CompilerParams(vmem_limit_bytes=VMEM_BYTES),
        cost_estimate=SMALL,
        name="wave",
    )(rank, *tables, *sources)


def level_kernel(
    step,
    rank_ref,
    count_ref,
    bus_hbm,
    cond_hbm,
    sat_hbm,
    volt_hbm,
    inject_hbm,
    there_ref,
    back_ref,
    zinv_ref,
    base_ref,
    sat_out,
    there_out,
    back_out,
    zinv_out,
    turned_out,
    bus_ref,
    cond_ref,
    sat_ref,
    volt_ref,
    inject_ref,
    sems,
):
    pairs = [
        (bus_hbm, bus_ref),
        (cond_hbm, cond_ref),
        (sat_hbm, sat_ref),
        (volt_hbm, volt_ref),
        (inject_hbm, inject_ref),
        (there_ref.at[rank_ref[0]], there_out),
        (back_ref.at[rank_ref[0]], back_out),
    ]
    pairs += [
        (zinv_ref.at[c, h], zinv_out.at[c, h])
        for h in range(zinv_ref.shape[1])
        for c in range(2)
    ]
    copies = [
        pltpu.make_async_copy(*pair, sems.at[q]) for q, pair in enumerate(pairs)
    ]
    for copy in copies:
        copy.start()
    for copy in copies[:3]:
        copy.wait()
    slots = bus_ref.shape[1]
    buses = volt_ref.shape[-1]
    total = jnp.zeros((16, buses), F32)
    for start in range(0, slots, step):
        at = pl.ds(start, step)
        slot_ids = lax.broadcasted_iota(jnp.int32, (1, step), 1) + start
        live = slot_ids < count_ref[0]
        pieces = []
        for ref in (cond_ref, sat_ref):
            rest = jnp.where(live, ref[:, at], 0.0)
            for _ in range(3):
                high = rest.astype(BF16).astype(F32)
                pieces.append(high)
                rest = rest - high
        pieces.append(jnp.zeros((10, step), F32))
        weights = jnp.concatenate(pieces, axis=0).astype(BF16)
        bus_ids = lax.broadcasted_iota(jnp.int32, (buses, step), 0)
        onehot = jnp.where(bus_ids == bus_ref[:, at], 1.0, 0.0).astype(BF16)
        total += lax.dot_general(
            weights, onehot, NT_DIMS, preferred_element_type=F32
        )
    cond = total[0:1] + total[1:2] + total[2:3]
    sat = total[3:4] + total[4:5] + total[5:6]
    sat_out[...] = jnp.broadcast_to(sat, sat_out.shape)
    for copy in copies[3:5]:
        copy.wait()
    for row in range(volt_ref.shape[0]):
        base_ref[row] = inject_ref[row] + cond * volt_ref[row]
    for copy in copies[5:7]:
        copy.wait()
    turned = turned_out.shape[2]
    for q, copy in enumerate(copies[7:]):
        copy.wait()
        turned_out[q % 2, q // 2] = zinv_out[q % 2, q // 2, :, :turned].T


def levels(rank, dev_count, dev_bus, dev_cond, dev_sat, volt, inject, tables, zinv, turned):
    slots = dev_bus.shape[1]
    buses = volt.shape[-1]
    step = 512 if slots % 512 == 0 else slots
    vmem = pl.BlockSpec(memory_space=pltpu.VMEM)
    smem = pl.BlockSpec(memory_space=pltpu.SMEM)
    anywhere = pl.BlockSpec(memory_space=pl.ANY)
    there, back = tables
    inputs = [
        pltpu.with_memory_space_constraint(each, pltpu.HBM)
        for each in (dev_bus, dev_cond, dev_sat, volt, inject, there, back)
    ] + [zinv]
    return pl.pallas_call(
        functools.partial(level_kernel, step),
        in_specs=[smem] * 2 + [anywhere] * len(inputs),
        out_specs=[vmem] * 6,
        out_shape=[
            pltpu.VMEM(volt.shape, F32),
            pltpu.VMEM((8, buses), F32),
            pltpu.VMEM(there.shape[1:], BF16),
            pltpu.VMEM(back.shape[1:], BF16),
            pltpu.VMEM(zinv.shape, BF16),
            pltpu.VMEM(zinv.shape[:2] + (turned, buses), BF16),
        ],
        scratch_shapes=[pltpu.VMEM(each.shape, each.dtype) for each in inputs[:5]]
        + [pltpu.SemaphoreType.DMA((len(inputs) + 2 * zinv.shape[1],))],
        compiler_params=pltpu.CompilerParams(vmem_limit_bytes=VMEM_BYTES),
        cost_estimate=SMALL,
        name="levels",
    )(rank, dev_count, *inputs)


def add_far(far, blocks, hot):
    for first in range(0, len(blocks), 2):
        parts = [split(block) for block in blocks[first : first + 2]]
        rows = slice(first * NBD, (first + len(parts)) * NBD)
        for piece in range(2):
            edges = jnp.concatenate([part[piece] for part in parts], axis=1)
            far += jnp.dot(edges, hot[rows], preferred_element_type=F32)
    return far


def tie_kernel(
    h_local, areas, origins, late_count, place_ref, *refs
):
    lists, refs = refs[:5], refs[5:]
    early = len(origins) - late_count
    blocks, refs = refs[:early], refs[early:]
    far_out, hot_out, adm_out, target_out = refs[:4]
    bus_ref, area_ref, far_ref, res_ref, reac_ref, held, sems = refs[4:]
    copies = [
        pltpu.make_async_copy(*pair, sems.at[q])
        for q, pair in enumerate(zip(lists, refs[4:9]))
    ]
    copies += [
        pltpu.make_async_copy(block, held.at[q], sems.at[5 + q])
        for q, block in enumerate(blocks)
    ]
    for copy in copies:
        copy.start()
    for copy in copies[:5]:
        copy.wait()
    ties = bus_ref.shape[1]
    edge_ids = lax.broadcasted_iota(jnp.int32, (NBD, ties), 0)
    far_hit = edge_ids == far_ref[...]
    hots = []
    for step, flip in origins:
        origin = (place_ref[1] + areas - step) % areas
        hit = area_ref[...] == (origin ^ 1 if flip else origin)
        hots.append(jnp.where(far_hit & hit, 1.0, 0.0).astype(BF16))
    hot_out[...] = jnp.concatenate(hots[early:], axis=0)
    target_out[...] = jnp.where(edge_ids == bus_ref[...], 1.0, 0.0).astype(BF16)
    resist = res_ref[...]
    for h in range(h_local):
        order = (2 * (place_ref[0] * h_local + h) + 1).astype(F32)
        reactance = reac_ref[...] * order
        denominator = resist * resist + reactance * reactance
        adm_out[pl.ds(h, 1), :] = resist / denominator
        adm_out[pl.ds(h_local + h, 1), :] = -reactance / denominator
    for copy in copies[5:]:
        copy.wait()
    far_out[...] = add_far(
        jnp.zeros(far_out.shape, F32),
        [held[q] for q in range(early)],
        jnp.concatenate(hots[:early], axis=0),
    )


def tie_parts(place, tie_lists, blocks, areas, origins, late_count, h_local):
    ties = tie_lists[0].shape[1]
    rows = blocks[0].shape[0]
    vmem = pl.BlockSpec(memory_space=pltpu.VMEM)
    return pl.pallas_call(
        functools.partial(tie_kernel, h_local, areas, origins, late_count),
        in_specs=[pl.BlockSpec(memory_space=pltpu.SMEM)]
        + [pl.BlockSpec(memory_space=pl.ANY)] * (len(tie_lists) + len(blocks)),
        out_specs=[vmem] * 4,
        out_shape=[
            pltpu.VMEM((rows, ties), F32),
            pltpu.VMEM((late_count * NBD, ties), BF16),
            pltpu.VMEM((2 * h_local, ties), F32),
            pltpu.VMEM((NBD, ties), BF16),
        ],
        scratch_shapes=[pltpu.VMEM(each.shape, each.dtype) for each in tie_lists]
        + [
            pltpu.VMEM((len(blocks), rows, NBD), F32),
            pltpu.SemaphoreType.DMA((len(blocks) + len(tie_lists),)),
        ],
        compiler_params=pltpu.CompilerParams(vmem_limit_bytes=VMEM_BYTES),
        cost_estimate=SMALL,
        name="ties",
    )(place, *tie_lists, *blocks)


def tie_currents(far, adm, target, scaled, h_local, scens):
    half = h_local * scens
    for h in range(h_local):
        adm_real, adm_imag = adm[h : h + 1], adm[h_local + h : h_local + h + 1]
        real = far[h * scens : (h + 1) * scens]
        imag = far[half + h * scens : half + (h + 1) * scens]
        scaled[pl.ds(h * scens, scens), :] = adm_real * real - adm_imag * imag
        scaled[pl.ds(half + h * scens, scens), :] = adm_real * imag + adm_imag * real
    high, low = split(scaled[...])
    return lax.dot_general(
        high, target, NT_DIMS, preferred_element_type=F32
    ) + lax.dot_general(low, target, NT_DIMS, preferred_element_type=F32)


def solve_kernel(start, width, ranks, late_count, place_ref, *refs):
    refs = list(refs)

    def take(count):
        taken, refs[:count] = refs[:count], []
        return taken

    base_ref, sat_ref, zinv_ref, _ = take(4)
    shaped_refs = take(ranks)
    last = late_count > 0
    if last:
        total_ref, far_ref, hot_ref, adm_ref, target_ref = take(5)
        blocks = take(late_count)
        out_ref, full, stage, sem, scaled = refs
    else:
        out_ref, mark_ref, full = refs
        mark_ref[...] = jnp.zeros(mark_ref.shape, F32)
        stage = out_ref
    _, h_local, scens, _ = base_ref.shape
    columns = shaped_refs[0].shape[0]
    part = scens // ranks
    for k, ref in enumerate(shaped_refs):
        quarter = pl.ds(pl.multiple_of((place_ref[0] ^ k) * part, 8), part)
        for j in range(columns):
            at = pl.ds(j * LANES, LANES)
            for row in range(2 * h_local):
                full[row, quarter, at] = ref[j, pl.ds(row * part, part), :]
    if last:
        far = add_far(far_ref[...], [block[...] for block in blocks], hot_ref[...])
        ties = tie_currents(
            far, adm_ref[...], target_ref[...], scaled, h_local, scens
        )
    lanes = pl.ds(start, width)
    sat = sat_ref[0:1, lanes]
    copies = []
    for h in range(h_local):
        parts = []
        for c in range(2):
            row = c * h_local + h
            rhs = base_ref[c, h, :, lanes] + sat * full[row]
            if last:
                here = ties[row * scens : (row + 1) * scens]
                if width > NBD:
                    rhs = jnp.concatenate([rhs[:, :NBD] + here, rhs[:, NBD:]], axis=1)
                else:
                    rhs = rhs + here
            parts.append(rhs.astype(BF16))
        both = jnp.concatenate(parts, axis=0)
        if last:
            by_real = jnp.dot(both, zinv_ref[0, h], preferred_element_type=F32)
            by_imag = jnp.dot(both, zinv_ref[1, h], preferred_element_type=F32)
        else:
            by_real = lax.dot_general(
                both, zinv_ref[0, h, :, lanes], NT_DIMS, preferred_element_type=F32
            )
            by_imag = lax.dot_general(
                both, zinv_ref[1, h, :, lanes], NT_DIMS, preferred_element_type=F32
            )
        real = by_real[:scens] - by_imag[scens:]
        imag = by_real[scens:] + by_imag[:scens]
        if last:
            real = real + total_ref[0, h]
            imag = imag + total_ref[1, h]
        stage[0, h] = real
        stage[1, h] = imag
        if last:
            copy = pltpu.make_async_copy(stage.at[:, h], out_ref.at[:, h], sem.at[h])
            copy.start()
            copies.append(copy)
    for copy in copies:
        copy.wait()


def solve(place, base, sat, zinvs, shaped, tie, start, width):
    _, h_local, scens, _ = base.shape
    ranks = len(shaped)
    vmem = pl.BlockSpec(memory_space=pltpu.VMEM)
    anywhere = pl.BlockSpec(memory_space=pl.ANY)
    operands = [base, sat, *zinvs, *shaped]
    in_specs = [vmem] * len(operands)
    scratch = [pltpu.VMEM((2 * h_local, scens, width), F32)]
    late = []
    if tie is not None:
        total, parts, late = tie
        rows, ties = parts[0].shape
        operands += [total, *parts, *late]
        in_specs += [vmem] * (1 + len(parts) + len(late))
        out_specs = anywhere
        out_shape = jax.ShapeDtypeStruct(base.shape, F32)
        scratch += [
            pltpu.VMEM(base.shape, F32),
            pltpu.SemaphoreType.DMA((h_local,)),
            pltpu.VMEM((rows, ties), F32),
        ]
    else:
        in_specs[3] = anywhere
        out_specs = [vmem, vmem]
        out_shape = [
            pltpu.VMEM(base.shape, F32),
            pltpu.VMEM((8, LANES), F32),
        ]
    return pl.pallas_call(
        functools.partial(solve_kernel, start, width, ranks, len(late)),
        in_specs=[pl.BlockSpec(memory_space=pltpu.SMEM)] + in_specs,
        out_specs=out_specs,
        out_shape=out_shape,
        scratch_shapes=scratch,
        compiler_params=pltpu.CompilerParams(vmem_limit_bytes=VMEM_BYTES),
        cost_estimate=SMALL,
        name="solve",
    )(place, *operands)


def per_device(
    volt,
    inject,
    zinv,
    dev_bus,
    dev_count,
    dev_cond,
    dev_sat,
    tie_bus,
    tie_area,
    tie_far,
    tie_res,
    tie_reac,
):
    _, _, h_local, scens, buses = volt.shape
    ranks = lax.axis_size("harm")
    areas = lax.axis_size("area")
    rank = lax.axis_index("harm")
    area = lax.axis_index("area")
    part = scens // ranks
    rows = 2 * h_local
    place = jnp.stack([rank, area]).astype(jnp.int32)
    there, back, _, m_pad = wave_tables(ranks, h_local)
    zinv = pltpu.with_memory_space_constraint(zinv[:, 0], pltpu.HBM)
    flat = volt.reshape(rows, scens, buses)

    def swap(value, k):
        return lax.ppermute(value, "harm", [(i, i ^ k) for i in range(ranks)])

    sizes = chunk_sizes(buses)
    starts = [buses - sum(sizes[: i + 1]) for i in range(len(sizes))]

    partners = tuple(range(ranks - 1, 1, -1))
    pieces = send_pieces(
        jnp.full((1,), rank, jnp.int32),
        pltpu.with_memory_space_constraint(flat, pltpu.HBM),
        partners,
        part,
    )
    flat_now, *pieces = lax.optimization_barrier((flat, *pieces))
    far = [swap(each, ranks - 1 - q) for q, each in enumerate(pieces)]
    sibling = swap(flat_now, 1)
    sources = [flat, sibling] + far[::-1]

    edge = volt[..., :NBD].reshape(rows * scens, NBD)

    def shift(value, step):
        return lax.ppermute(
            value, "area", [(a, (a + step) % areas) for a in range(areas)]
        )

    def exchange(value):
        return lax.ppermute(value, "area", [(a, a ^ 1) for a in range(areas)])

    edge = after(edge, *pieces)
    blocks = [edge, exchange(edge)]
    base, sat, there, back, held, turned = levels(
        place,
        dev_count,
        after(dev_bus, sibling),
        dev_cond,
        dev_sat,
        flat,
        inject.reshape(flat.shape),
        (jnp.asarray(there), jnp.asarray(back)),
        zinv,
        sizes[-1],
    )
    def run_wave(index):
        return wave(
            place,
            (there, back),
            m_pad,
            sources,
            part,
            starts[index],
            sizes[index],
        )

    waves = [list(run_wave(index)) for index in range(len(sizes))]
    ring = {2: shift(edge, 2)}
    if areas > 4:
        ring[areas - 2] = shift(edge, areas - 2)
    for step in range(4, areas - 2, 2):
        ring[step] = shift(after(ring[step - 2], ring[areas - 2], sat), 2)
    late = []
    origins, late_origins = [(0, 0), (0, 1)], []
    for step, block in ring.items():
        blocks.append(block)
        origins.append((step, 0))
        if step == 2:
            blocks.append(exchange(after(block, blocks[1], far[0], sat)))
            origins.append((step, 1))
        else:
            needs = blocks[3:4] if step == areas - 2 else [waves[-1][0]]
            late.append(exchange(after(block, *needs)))
            late_origins.append((step, 1))

    base = base.reshape(2, h_local, scens, buses)
    tie_lists = [
        pltpu.with_memory_space_constraint(each, pltpu.HBM)
        for each in (tie_bus, tie_area[:, :, 0], tie_far, tie_res, tie_reac)
    ]
    parts = tie_parts(
        place, tie_lists, blocks, areas, origins + late_origins, len(late), h_local
    )

    shaped = []
    for index, outs in enumerate(waves):
        got = [outs[0]] + [swap(outs[k], k) for k in range(1, ranks - 1)]
        if index == len(waves) - 1:
            outs[-1] = after(outs[-1], parts[0], got[1])
        shaped.append(got + [swap(outs[-1], ranks - 1)])
    total, mark = solve(
        place, base, sat, (held, zinv), shaped[0], None, starts[0], sizes[0]
    )
    total = solve(
        place,
        base,
        sat,
        (turned, mark),
        shaped[1],
        (total, parts, late),
        starts[1],
        sizes[1],
    )
    return total[:, None]


def solution(mesh):
    wide = P(None, "area", "harm", None, None)
    flat = P("area", None)
    in_specs = (
        wide,
        wide,
        wide,
        flat,
        P("area"),
        flat,
        flat,
        flat,
        P("area", None, None),
        flat,
        flat,
        flat,
    )
    return jax.shard_map(
        per_device, mesh=mesh, in_specs=in_specs, out_specs=wide, check_vma=False
    )
```
